128 devices in a mesh: dp: 16 (over y_hi, x, core), space: 8 (over z, y_lo).
Axes of the slice: x: 4, y: 4 (y_hi: 2, y_lo: 2; y = y_hi * 2 + y_lo), z: 4, core: 2. Of those that a mesh axis runs over, the one named last changes fastest.
Arguments:
- volume: bfloat16 [16, 32, 32, 128], P('dp', 'space'), may hold values from -6 to 6
- first_kernel: bfloat16 [3, 3, 3, 4, 64], replicated, may hold values from -0.625 to 0.625
- mid_kernel: bfloat16 [3, 3, 3, 64, 128], replicated, may hold values from -0.15625 to 0.15625
- deep_kernel: bfloat16 [3, 3, 3, 128, 256], replicated, may hold values from -0.109375 to 0.109375
- deep_cotangent: bfloat16 [16, 16, 16, 16, 256], P('dp', 'space'), may hold values from -6 to 6
Outputs:
- deep_output: bfloat16 [16, 16, 16, 16, 256], P('dp', 'space')
- deep_kernel_grad: float32 [3, 3, 3, 128, 256], P(None, None, None, 'space')
- mid_kernel_grad: float32 [3, 3, 3, 64, 128], replicated
The draws below stay inside these ranges and needn't reach their ends.
All inputs are finite; a program needn't handle non-finite values.
Results may differ from the reference program's by a relative error of at most 0.024.
Values may be sent and summed in bfloat16 or wider, within the bound.
A program may use at most 128 MiB of HBM per device.

```python
import math
import jax
import jax.numpy as jnp
from jax import lax

CIN = 4
C1 = 64
C2 = 128
C3 = 256
HW = 32
BATCH = 16
DEPTH = 32


def levels(key, extent, pieces, low, top_value):
    level = 1.0
    for dim, shards_of in pieces:
        steps = jax.random.uniform(jax.random.fold_in(jax.random.fold_in(key, 6), dim), (shards_of,), jnp.float32, low / len(pieces), top_value / len(pieces))
        level = level * jnp.repeat(jnp.exp(steps), extent[dim] // shards_of).reshape((-1,) + (1,) * (len(extent) - 1 - dim))
    return level


def centred(rng, extent, spread, most, shards=(), dtype=jnp.bfloat16):
    result = jax.random.normal(rng, extent, jnp.float32) * spread
    if len(shards) > 0:
        result = levels(rng, extent, shards, -0.22, 0.18) * result
    return jnp.clip(result, min=-most, max=most).astype(dtype)


def setup_inputs(seed: int = 0) -> dict:
    splits = jax.random.split(jax.random.key(seed), 6)
    return {
        "volume": centred(splits[0], (BATCH, DEPTH, HW, HW * CIN), 1.0, 6.0, ((0, 16), (1, 8))),
        "first_kernel": centred(splits[1], (3, 3, 3, CIN, C1), (27 * CIN) ** -0.5, 0.625),
        "mid_kernel": centred(splits[2], (3, 3, 3, C1, C2), (27 * C1) ** -0.5, 0.15625),
        "deep_kernel": centred(splits[3], (3, 3, 3, C2, C3), (27 * C2) ** -0.5, 0.109375),
        "deep_cotangent": centred(splits[4], (BATCH, DEPTH // 2, HW // 2, HW // 2, C3), 1.0, 6.0, ((0, 16), (1, 8))),
    }


SLOPE = 0.3
HIGH = lax.Precision.HIGHEST

def activate(value):
    return SLOPE * value + (1.0 - SLOPE) * value * jax.nn.sigmoid(value)

def activate_slope(value):
    sig = jax.nn.sigmoid(value)
    return SLOPE + (1.0 - SLOPE) * (sig + value * sig * (1.0 - sig))

def convolve(values, kernel):
    return lax.conv_general_dilated(values[None], kernel, (1, 1, 1), [(1, 1), (1, 1), (1, 1)], dimension_numbers=('NDHWC', 'DHWIO', 'NDHWC'), precision=HIGH)[0]

def pool_cells(values):
    dd, hh, ww, cc = values.shape
    return values.reshape(dd // 2, 2, hh // 2, 2, ww // 2, 2, cc).mean(axis=(1, 3, 5))

def expand(values):
    return jnp.repeat(jnp.repeat(jnp.repeat(values, 2, 0), 2, 1), 2, 2)

def kernel_grad(padded, cotangent):
    dd, hh, ww, _ = cotangent.shape
    tap_list = []
    for depth_off in range(3):
        for row_off in range(3):
            for col_off in range(3):
                window = padded[depth_off:depth_off + dd, row_off:row_off + hh, col_off:col_off + ww]
                tap_list.append(jnp.einsum('dhwi,dhwo->io', window, cotangent, precision=HIGH))
    return jnp.stack(tap_list).reshape(3, 3, 3, padded.shape[-1], cotangent.shape[-1])

def pad_cells(values):
    return jnp.pad(values, ((1, 1), (1, 1), (1, 1), (0, 0)))

def one_sample(sample, cotangent, first_f, mid_f, deep_f):
    field_in = sample.reshape(DEPTH, HW, HW, CIN).astype(jnp.float32)
    hidden = activate(convolve(field_in, first_f)).astype(jnp.bfloat16)
    pre_mid = convolve(hidden.astype(jnp.float32), mid_f)
    pooled = pool_cells(activate(pre_mid)).astype(jnp.bfloat16)
    pre_deep = convolve(pooled.astype(jnp.float32), deep_f)
    output = activate(pre_deep).astype(jnp.bfloat16)
    grad_pre = (cotangent.astype(jnp.float32) * activate_slope(pre_deep)).astype(jnp.bfloat16)
    deep_term = kernel_grad(pad_cells(pooled.astype(jnp.float32)), grad_pre.astype(jnp.float32))
    flipped = jnp.swapaxes(deep_f[::-1, ::-1, ::-1], 3, 4)
    pooled_grad = convolve(grad_pre.astype(jnp.float32), flipped).astype(jnp.bfloat16)
    grad_mid = (expand(pooled_grad.astype(jnp.float32)) * 0.125 * activate_slope(pre_mid)).astype(jnp.bfloat16)
    mid_term = kernel_grad(pad_cells(hidden.astype(jnp.float32)), grad_mid.astype(jnp.float32))
    return (output, deep_term, mid_term)

def reference(volume, first_kernel, mid_kernel, deep_kernel, deep_cotangent):
    first_f = first_kernel.astype(jnp.float32)
    mid_f = mid_kernel.astype(jnp.float32)
    deep_f = deep_kernel.astype(jnp.float32)

    def sample_step(carry, pair):
        output, deep_term, mid_term = one_sample(pair[0], pair[1], first_f, mid_f, deep_f)
        return ((carry[0] + deep_term, carry[1] + mid_term), output)
    start_sums = (jnp.zeros(deep_kernel.shape, jnp.float32), jnp.zeros(mid_kernel.shape, jnp.float32))
    sums, outputs = lax.scan(sample_step, start_sums, (volume, deep_cotangent))
    deep_scale = math.sqrt(BATCH * (DEPTH // 2) * (HW // 2) * (HW // 2))
    mid_scale = math.sqrt(BATCH * DEPTH * HW * HW)
    return (outputs, sums[0] / deep_scale, sums[1] / mid_scale)
```

```python
import functools
import math

import jax
import jax.numpy as jnp
from jax import lax
from jax.experimental import pallas as pl
from jax.experimental.pallas import tpu as pltpu
from jax.sharding import PartitionSpec as P

SLOPE = 0.3
BF = jnp.bfloat16
F32 = jnp.float32
MESH = pl.DeviceIdType.MESH

NS = 8
NQ = 8
CS = 128 // NS
DROWS = 27 * CS
DPIECE = 64
MHALF = 896
MPIECE = MHALF // NS


def sigmoid(z):
    return 0.5 * jnp.tanh(0.5 * z) + 0.5


def act(z):
    return z * (SLOPE + (1.0 - SLOPE) * sigmoid(z))


def act_slope(z):
    s = sigmoid(z)
    return SLOPE + (1.0 - SLOPE) * (s + z * s * (1.0 - s))


def dot(a, b, dims=((1,), (0,))):
    return lax.dot_general(a, b, (dims, ((), ())), preferred_element_type=F32)


def kernel(
    vol_ref, e_ref, km_ref, kd_ref, cot_ref,
    out_ref, dk_ref, mk_ref,
    vhalo, vf, volb, tmat, ybuf, yst, wmid, xpad, xt, slope_mid,
    phalo, pf, pcat, pt, pooled_send, predeep, grad, ghalo, gcat, dbuf, drecv1, dsum1,
    drecv2, dsum2, drecv3, dfull, dother, gmid, mbuf, mrecv1, msum1, mrecv2,
    mrecv3, mfull, mout,
    halo_send, halo_recv, pair_send, pair_recv, ds_send, ds_recv, dq_send, dq_recv,
    dg_send, dg_recv, ms_send, ms_recv, mq_send, mq_recv, mg_send, mg_recv,
):
    s = lax.axis_index("space")
    d = lax.axis_index("dp")
    q = d // 2
    core = d % 2
    other = d + 1 - 2 * core

    def space_peer(k):
        return lax.rem(s + k, NS)

    def dp_peer(k):
        return lax.rem(q + k, NQ) * 2 + core

    up = space_peer(1)
    down = space_peer(NS - 1)

    barrier = pltpu.get_barrier_semaphore()
    for k in range(1, NS):
        pl.semaphore_signal(barrier, inc=1, device_id={"space": space_peer(k)}, device_id_type=MESH)
    for k in range(1, NQ):
        pl.semaphore_signal(barrier, inc=1, device_id={"dp": dp_peer(k)}, device_id_type=MESH)
    pl.semaphore_signal(barrier, inc=1, device_id={"dp": other}, device_id_type=MESH)

    def send(src, dst, ssem, rsem, device):
        copy = pltpu.make_async_remote_copy(
            src_ref=src, dst_ref=dst, send_sem=ssem, recv_sem=rsem,
            device_id=device, device_id_type=MESH,
        )
        copy.start()
        return copy

    def zero_t(i, c):
        tmat[pl.ds(i * 16, 16), :] = jnp.zeros((16, 2048), BF)
        return c

    lax.fori_loop(0, 72, zero_t, 0)
    for ab in range(9):
        base = ab * 128
        for m in range(8):
            lo = slice(2 * m * 128, 2 * m * 128 + 128)
            hi = slice(2 * m * 128 + 128, 2 * m * 128 + 256)
            if m > 0:
                tmat[base + 16 * (m - 1) : base + 16 * m, lo] = e_ref[ab, 0]
            tmat[base + 16 * m : base + 16 * m + 16, lo] = e_ref[ab, 1]
            tmat[base + 16 * m : base + 16 * m + 16, hi] = e_ref[ab, 2]
            if m < 7:
                tmat[base + 16 * (m + 1) : base + 16 * (m + 2), hi] = e_ref[ab, 3]

    for ab in range(9):
        k0 = km_ref[(ab * 3) * 64 : (ab * 3 + 1) * 64, :]
        k1 = km_ref[(ab * 3 + 1) * 64 : (ab * 3 + 2) * 64, :]
        k2 = km_ref[(ab * 3 + 2) * 64 : (ab * 3 + 3) * 64, :]
        z = jnp.zeros((64, 128), BF)
        base = ab * 256
        wmid[base : base + 64, 0:128] = k1
        wmid[base : base + 64, 128:256] = k0
        wmid[base + 64 : base + 128, 0:128] = k2
        wmid[base + 64 : base + 128, 128:256] = k1
        wmid[base + 128 : base + 192, 0:128] = z
        wmid[base + 128 : base + 192, 128:256] = k2
        wmid[base + 192 : base + 256, 0:128] = k0
        wmid[base + 192 : base + 256, 128:256] = z
    for i in range(6):
        xpad[i, 0:16, :] = jnp.zeros((16, 256), BF)
        xpad[i, 528:544, :] = jnp.zeros((16, 256), BF)
    for i in range(4):
        pcat[i, 0:16, :] = jnp.zeros((16, 384), BF)
        pcat[i, 272:288, :] = jnp.zeros((16, 384), BF)
        gcat[i, 0:16, :] = jnp.zeros((16, 768), BF)
        gcat[i, 272:288, :] = jnp.zeros((16, 768), BF)

    pl.semaphore_wait(barrier, NS - 1 + NQ - 1 + 1)

    v_down = send(vol_ref.at[0:2], vhalo.at[1], halo_send.at[0], halo_recv.at[0], {"space": down})
    v_up = send(vol_ref.at[2:4], vhalo.at[0], halo_send.at[1], halo_recv.at[1], {"space": up})
    v_down.wait()
    v_up.wait()

    vf[0:8, :] = jnp.zeros((8, 128), F32)
    vf[264:272, :] = jnp.zeros((8, 128), F32)
    low = jnp.where(s == 0, 0.0, vhalo[0].astype(F32))
    high = jnp.where(s == NS - 1, 0.0, vhalo[1].astype(F32))
    vf[8:72, :] = low.reshape(64, 128)
    vf[72:200, :] = vol_ref[...].astype(F32).reshape(128, 128)
    vf[200:264, :] = high.reshape(64, 128)
    vrow = lax.broadcasted_iota(jnp.int32, (256, 128), 0) % 32
    volb[0] = jnp.where(vrow == 0, 0.0, vf[7:263, :]).astype(BF)
    volb[1] = vf[8:264, :].astype(BF)
    volb[2] = jnp.where(vrow == 31, 0.0, vf[9:265, :]).astype(BF)

    def first(m, c):
        lhs = jnp.concatenate(
            [volb[b, 32 * a : 32 * a + 192, :] for a in range(3) for b in range(3)], axis=1
        )
        col = pl.multiple_of(m * 256, 256)
        ybuf[:, pl.ds(col, 256)] = act(dot(lhs, tmat[:, pl.ds(col, 256)]))
        return c

    lax.fori_loop(0, 8, first, 0)
    ybuf[0:32, :] = jnp.where(s == 0, 0.0, ybuf[0:32, :])
    ybuf[160:192, :] = jnp.where(s == NS - 1, 0.0, ybuf[160:192, :])

    lane = lax.broadcasted_iota(jnp.int32, (32, 128), 1)
    zero = jnp.zeros((32, 128), F32)
    for i in range(6):
        ys = [ybuf[32 * i : 32 * i + 32, 128 * j : 128 * j + 128] for j in range(16)]
        for j in range(16):
            after = ys[j + 1] if j < 15 else zero
            before = ys[j - 1] if j > 0 else zero
            yst[0, pl.ds(j, 32, stride=16), :] = ys[j]
            yst[1, pl.ds(j, 32, stride=16), :] = jnp.where(lane < 64, after, before)
        xpad[i, 16:528, 0:128] = yst[0].astype(BF)
        xpad[i, 16:528, 128:256] = yst[1].astype(BF)

    prow = lax.broadcasted_iota(jnp.int32, (256, 128), 0) % 16
    pf[0:8, :] = jnp.zeros((8, 256), F32)
    pf[264:272, :] = jnp.zeros((8, 256), F32)

    def put_pooled(i, value):
        pf[8:264, 0:128] = value
        pcat[i, 16:272, 0:128] = jnp.where(prow == 0, 0.0, pf[7:263, 0:128]).astype(BF)
        pcat[i, 16:272, 128:256] = value.astype(BF)
        pcat[i, 16:272, 256:384] = jnp.where(prow == 15, 0.0, pf[9:265, 0:128]).astype(BF)

    def mid_plane(i):
        lhs = jnp.concatenate(
            [xpad[i + a, 16 * b : 16 * b + 512, :] for a in range(3) for b in range(3)], axis=1
        )
        pre = dot(lhs, wmid[...])
        slope_mid[i] = 0.125 * act_slope(pre)
        value = act(pre).reshape(16, 2, 16, 256)
        value = value[:, 0] + value[:, 1]
        return (value[:, :, :128] + value[:, :, 128:]).reshape(256, 128)

    p_copies = []
    for plane in range(2):
        pooled = ((mid_plane(2 * plane) + mid_plane(2 * plane + 1)) * 0.125).astype(BF)
        pooled_send[plane] = pooled
        p_copies.append(
            send(
                pooled_send.at[plane], phalo.at[1 - plane], halo_send.at[2 + plane],
                halo_recv.at[2 + plane], {"space": down if plane == 0 else up},
            )
        )
        put_pooled(plane + 1, pooled.astype(F32))

    def deep_taps(plane, a):
        lhs = jnp.concatenate(
            [pcat[plane + a, 16 * b : 16 * b + 256, :] for b in range(3)], axis=1
        )
        return dot(lhs, kd_ref[a * 1152 : (a + 1) * 1152, :])

    predeep[0] = deep_taps(0, 1) + deep_taps(0, 2)
    predeep[1] = deep_taps(1, 0) + deep_taps(1, 1)

    for b in range(3):
        for i in range(6):
            xt[b * 256 : (b + 1) * 256, i * 512 : (i + 1) * 512] = xpad[i, 16 * b : 16 * b + 512, :].T

    for copy in p_copies:
        copy.wait()
    put_pooled(0, jnp.where(s == 0, 0.0, phalo[0].astype(F32)))
    put_pooled(3, jnp.where(s == NS - 1, 0.0, phalo[1].astype(F32)))

    g_copies = []
    for plane in range(2):
        pre = predeep[plane] + deep_taps(plane, 0 if plane == 0 else 2)
        out_ref[plane] = act(pre).astype(BF)
        grad[plane] = (cot_ref[plane].astype(F32) * act_slope(pre)).astype(BF)
        g_copies.append(
            send(
                grad.at[plane], ghalo.at[1 - plane], halo_send.at[4 + plane],
                halo_recv.at[4 + plane], {"space": down if plane == 0 else up},
            )
        )

    grow = lax.broadcasted_iota(jnp.int32, (256, 256), 0) % 16

    def put_grad(i, value):
        pf[8:264, :] = value
        gcat[i, 16:272, 0:256] = jnp.where(grow == 15, 0.0, pf[9:265, :]).astype(BF)
        gcat[i, 16:272, 256:512] = value.astype(BF)
        gcat[i, 16:272, 512:768] = jnp.where(grow == 0, 0.0, pf[7:263, :]).astype(BF)

    put_grad(1, grad[0].astype(F32))
    put_grad(2, grad[1].astype(F32))

    for b in range(3):
        for i in range(4):
            pt[b * 384 : (b + 1) * 384, i * 256 : (i + 1) * 256] = pcat[i, 16 * b : 16 * b + 256, :].T
    gown = grad[...].reshape(512, 256)
    for a in range(3):
        term = dot(pt[:, a * 256 : a * 256 + 512], gown).astype(BF).reshape(9, 128, 256)
        dbuf[0, 9 * a : 9 * a + 9] = term[:, :, :128]
        dbuf[1, 9 * a : 9 * a + 9] = term[:, :, 128:]
    d_pair = send(dbuf.at[1 - core], drecv1, pair_send.at[0], pair_recv.at[0], {"dp": other})

    for copy in g_copies:
        copy.wait()
    put_grad(0, jnp.where(s == 0, 0.0, ghalo[0].astype(F32)))
    put_grad(3, jnp.where(s == NS - 1, 0.0, ghalo[1].astype(F32)))

    def back_plane(plane):
        total = None
        for a in range(3):
            for b in range(3):
                for c in range(3):
                    rows = 16 * (2 - b)
                    tap = (a * 3 + b) * 3 + c
                    term = dot(
                        gcat[plane + 2 - a, rows : rows + 256, 256 * c : 256 * c + 256],
                        kd_ref[tap * 128 : (tap + 1) * 128, :],
                        ((1,), (1,)),
                    )
                    total = term if total is None else total + term
        return total.astype(BF).astype(F32)

    back = [back_plane(0)]

    d_pair.wait()
    dsum1[...] = (dbuf[core].astype(F32) + drecv1[...].astype(F32)).astype(BF)
    d_space = []
    for k in range(1, NS):
        row = pl.multiple_of(space_peer(k) * CS, CS)
        d_space.append(
            send(
                dsum1.at[:, pl.ds(row, CS), :], drecv2.at[k], ds_send.at[k], ds_recv.at[k],
                {"space": space_peer(k)},
            )
        )
    back.append(back_plane(1))

    for plane in range(2):
        wide = jnp.concatenate([back[plane], back[plane]], axis=1).reshape(16, 1, 16, 256)
        for i in range(2):
            value = slope_mid[2 * plane + i].reshape(16, 2, 16, 256) * wide
            row = (2 * plane + i) * 512
            gmid[row : row + 512, :] = value.reshape(512, 256).astype(BF)

    mbuf[27 * 64 : 28 * 64, :] = jnp.zeros((64, 128), BF)

    def mid_grad(a):
        part = dot(xt[:, a * 512 : a * 512 + 2048], gmid[...])
        for b in range(3):
            r = part[b * 256 : (b + 1) * 256]
            row = (a * 3 + b) * 192
            mbuf[row : row + 64, :] = (r[0:64, 128:] + r[192:256, :128]).astype(BF)
            mbuf[row + 64 : row + 128, :] = (r[0:64, :128] + r[64:128, 128:]).astype(BF)
            mbuf[row + 128 : row + 192, :] = (r[64:128, :128] + r[128:192, 128:]).astype(BF)

    mid_grad(0)

    for copy in d_space:
        copy.wait()
    own_row = pl.multiple_of(s * CS, CS)
    total = dsum1[:, pl.ds(own_row, CS), :].astype(F32)
    for k in range(1, NS):
        total = total + drecv2[k].astype(F32)
    dsum2[0:DROWS, :] = total.reshape(DROWS, 128).astype(BF)
    dsum2[DROWS : NQ * DPIECE, :] = jnp.zeros((NQ * DPIECE - DROWS, 128), BF)
    d_dp = []
    for k in range(1, NQ):
        row = pl.multiple_of(lax.rem(q + k, NQ) * DPIECE, DPIECE)
        d_dp.append(
            send(
                dsum2.at[pl.ds(row, DPIECE), :], drecv3.at[k], dq_send.at[k], dq_recv.at[k],
                {"dp": dp_peer(k)},
            )
        )

    mid_grad(1)

    for copy in d_dp:
        copy.wait()
    q_row = pl.multiple_of(q * DPIECE, DPIECE)
    total = dsum2[pl.ds(q_row, DPIECE), :].astype(F32)
    for k in range(1, NQ):
        total = total + drecv3[k].astype(F32)
    dfull[pl.ds(q_row, DPIECE), :] = total.astype(BF)
    d_gather = []
    for k in range(1, NQ):
        d_gather.append(
            send(
                dfull.at[pl.ds(q_row, DPIECE), :], dfull.at[pl.ds(q_row, DPIECE), :],
                dg_send.at[k], dg_recv.at[k], {"dp": dp_peer(k)},
            )
        )

    mid_grad(2)

    m_mine = pl.multiple_of(core * MHALF, MHALF)
    m_theirs = pl.multiple_of((1 - core) * MHALF, MHALF)
    m_pair = send(
        mbuf.at[pl.ds(m_theirs, MHALF), :], mrecv1, pair_send.at[1], pair_recv.at[1], {"dp": other}
    )
    for copy in d_gather:
        copy.wait()
    d_last = send(dfull, dother, pair_send.at[2], pair_recv.at[2], {"dp": other})
    m_pair.wait()
    msum1[...] = (mbuf[pl.ds(m_mine, MHALF), :].astype(F32) + mrecv1[...].astype(F32)).astype(BF)
    m_space = []
    for k in range(1, NS):
        row = pl.multiple_of(space_peer(k) * MPIECE, MPIECE)
        m_space.append(
            send(
                msum1.at[pl.ds(row, MPIECE), :], mrecv2.at[k], ms_send.at[k], ms_recv.at[k],
                {"space": space_peer(k)},
            )
        )
    d_last.wait()
    mine = dfull[0:DROWS, :]
    theirs = dother[0:DROWS, :]
    dk_ref[:, 0:128] = jnp.where(core == 0, mine, theirs)
    dk_ref[:, 128:256] = jnp.where(core == 0, theirs, mine)
    for copy in m_space:
        copy.wait()
    row = pl.multiple_of(s * MPIECE, MPIECE)
    total = msum1[pl.ds(row, MPIECE), :].astype(F32)
    for k in range(1, NS):
        total = total + mrecv2[k].astype(F32)
    mrecv3[q] = total.astype(BF)
    m_dp = []
    for k in range(1, NQ):
        m_dp.append(
            send(mrecv3.at[q], mrecv3.at[q], mq_send.at[k], mq_recv.at[k], {"dp": dp_peer(k)})
        )
    for copy in m_dp:
        copy.wait()
    total = mrecv3[0].astype(F32)
    for k in range(1, NQ):
        total = total + mrecv3[k].astype(F32)
    mfull[pl.ds(row, MPIECE), :] = total.astype(BF)
    m_gather = []
    for k in range(1, NS):
        m_gather.append(
            send(
                mfull.at[pl.ds(row, MPIECE), :], mfull.at[pl.ds(row, MPIECE), :],
                mg_send.at[k], mg_recv.at[k], {"space": space_peer(k)},
            )
        )
    for copy in m_gather:
        copy.wait()
    last = send(
        mfull, mout, pair_send.at[3], pair_recv.at[3], {"dp": other}
    )
    mk_ref[pl.ds(m_mine, MHALF), :] = mfull[...]
    last.wait()
    mk_ref[pl.ds(m_theirs, MHALF), :] = mout[...]


def on_device(volume, first_kernel, mid_kernel, deep_kernel, deep_cotangent):
    k = first_kernel.reshape(9, 3, 4, 64)
    pads = ((0, 0), (0, 0), (0, 0))
    even = jnp.pad(k, (pads[0], (0, 1), *pads[:2]))
    odd = jnp.pad(k, (pads[0], (1, 0), *pads[:2]))
    block = jnp.stack([even, odd], axis=3).reshape(9, 16, 128)
    tiles = jnp.stack(
        [
            jnp.pad(block[:, :4], ((0, 0), (12, 0), (0, 0))),
            jnp.pad(block[:, 4:], ((0, 0), (0, 4), (0, 0))),
            jnp.pad(block[:, :12], ((0, 0), (4, 0), (0, 0))),
            jnp.pad(block[:, 12:], ((0, 0), (0, 12), (0, 0))),
        ],
        axis=1,
    )
    vm = pl.BlockSpec(memory_space=pltpu.VMEM)
    dma = pltpu.SemaphoreType.DMA
    deep_out, deep_grad, mid_grad = pl.pallas_call(
        kernel,
        out_shape=(
            jax.ShapeDtypeStruct((2, 256, 256), BF),
            jax.ShapeDtypeStruct((DROWS, 256), BF),
            jax.ShapeDtypeStruct((2 * MHALF, 128), BF),
        ),
        in_specs=[vm] * 5,
        out_specs=(vm, vm, vm),
        scratch_shapes=[
            pltpu.VMEM((2, 2, 32, 128), BF),
            pltpu.VMEM((272, 128), F32),
            pltpu.VMEM((3, 256, 128), BF),
            pltpu.VMEM((1152, 2048), BF),
            pltpu.VMEM((192, 2048), F32),
            pltpu.VMEM((2, 512, 128), F32),
            pltpu.VMEM((2304, 256), BF),
            pltpu.VMEM((6, 544, 256), BF),
            pltpu.VMEM((768, 3072), BF),
            pltpu.VMEM((4, 512, 256), F32),
            pltpu.VMEM((2, 256, 128), BF),
            pltpu.VMEM((272, 256), F32),
            pltpu.VMEM((4, 288, 384), BF),
            pltpu.VMEM((1152, 1024), BF),
            pltpu.VMEM((2, 256, 128), BF),
            pltpu.VMEM((2, 256, 256), F32),
            pltpu.VMEM((2, 256, 256), BF),
            pltpu.VMEM((2, 256, 256), BF),
            pltpu.VMEM((4, 288, 768), BF),
            pltpu.VMEM((2, 27, 128, 128), BF),
            pltpu.VMEM((27, 128, 128), BF),
            pltpu.VMEM((27, 128, 128), BF),
            pltpu.VMEM((NS, 27, CS, 128), BF),
            pltpu.VMEM((NQ * DPIECE, 128), BF),
            pltpu.VMEM((NQ, DPIECE, 128), BF),
            pltpu.VMEM((NQ * DPIECE, 128), BF),
            pltpu.VMEM((NQ * DPIECE, 128), BF),
            pltpu.VMEM((2048, 256), BF),
            pltpu.VMEM((2 * MHALF, 128), BF),
            pltpu.VMEM((MHALF, 128), BF),
            pltpu.VMEM((MHALF, 128), BF),
            pltpu.VMEM((NS, MPIECE, 128), BF),
            pltpu.VMEM((NQ, MPIECE, 128), BF),
            pltpu.VMEM((MHALF, 128), BF),
            pltpu.VMEM((MHALF, 128), BF),
            dma((6,)), dma((6,)), dma((4,)), dma((4,)),
            *[dma((8,)) for _ in range(12)],
        ],
        compiler_params=pltpu.CompilerParams(
            collective_id=0, has_side_effects=True, vmem_limit_bytes=60 * 1024 * 1024
        ),
    )(
        volume[0],
        tiles,
        mid_kernel.reshape(27 * 64, 128),
        deep_kernel.reshape(27 * 128, 256),
        deep_cotangent.reshape(2, 256, 256),
    )
    deep_scale = math.sqrt(NQ * 2 * NS * 2 * 256)
    mid_scale = math.sqrt(NQ * 2 * NS * 4 * 1024)
    return (
        deep_out.reshape(1, 2, 16, 16, 256),
        deep_grad.astype(F32).reshape(3, 3, 3, CS, 256) / deep_scale,
        mid_grad[: 27 * 64].astype(F32).reshape(3, 3, 3, 64, 128) / mid_scale,
    )


def solution(mesh):
    in_specs = (P("dp", "space", None, None), P(), P(), P(), P("dp", "space", None, None, None))
    out_specs = (P("dp", "space", None, None, None), P(None, None, None, "space", None), P())
    return jax.shard_map(
        on_device, mesh=mesh, in_specs=in_specs, out_specs=out_specs, check_vma=False
    )
```

```python
import functools
import math

import jax
import jax.numpy as jnp
from jax import lax
from jax.experimental import pallas as pl
from jax.experimental.pallas import tpu as pltpu
from jax.sharding import PartitionSpec as P

SLOPE = 0.3
BF = jnp.bfloat16
F32 = jnp.float32
MESH = pl.DeviceIdType.MESH

NS = 8
NQ = 8
CS = 128 // NS
DROWS = 27 * CS
DPIECE = 64
MROWS = 28 * 64
MHALF = MROWS // 2
MPARTS = ((0, 512), (512, 512), (1024, 768))
MONE = MHALF // NS


def sigmoid(z):
    return 0.5 * jnp.tanh(0.5 * z) + 0.5


def act(z):
    return z * (SLOPE + (1.0 - SLOPE) * sigmoid(z))


def act_slope(z):
    s = sigmoid(z)
    return SLOPE + (1.0 - SLOPE) * (s + z * s * (1.0 - s))


def dot(a, b, dims=((1,), (0,))):
    return lax.dot_general(a, b, (dims, ((), ())), preferred_element_type=F32)


def kernel(
    fk_ref, vol_hbm, km_hbm, kd_hbm, cot_hbm,
    out_ref, dk_ref, mk_ref,
    vol_ref, km_ref, kd_ref, cot_ref,
    vhalo, ef, vf, volb, tmat, ybuf, yst, wmid, xpad, xt, pre_mid, slope_mid,
    phalo, pf, pcat, pt, pooled_send, predeep, grad, bsend, bhalo, gcat, dbuf, drecv1, dsum1,
    drecv2, dsum2, drecv3, dfull, dother, gmid, mbuf, mrecv1, msum1, mrecv2,
    mrecv3, mfull, mout,
    load_sem, halo_send, halo_recv, pair_send, pair_recv, ds_send, ds_recv, dq_send, dq_recv,
    dg_send, dg_recv, mp_send, mp_recv, ms_send, ms_recv, mq_send, mq_recv, mg_send, mg_recv,
    mo_send, mo_recv,
):
    s = lax.axis_index("space")
    d = lax.axis_index("dp")
    q = d // 2
    core = d % 2
    other = d + 1 - 2 * core

    def space_peer(k):
        return lax.rem(s + k, NS)

    def dp_peer(k):
        return lax.rem(q + k, NQ) * 2 + core

    up = space_peer(1)
    down = space_peer(NS - 1)

    barrier = pltpu.get_barrier_semaphore()
    for k in (1, NS - 1, *range(2, NS - 1)):
        pl.semaphore_signal(barrier, inc=1, device_id={"space": space_peer(k)}, device_id_type=MESH)
    for k in range(1, NQ):
        pl.semaphore_signal(barrier, inc=1, device_id={"dp": dp_peer(k)}, device_id_type=MESH)
    pl.semaphore_signal(barrier, inc=1, device_id={"dp": other}, device_id_type=MESH)

    loads = []
    for i, (src, dst) in enumerate(
        ((vol_hbm, vol_ref), (km_hbm, km_ref), (kd_hbm, kd_ref), (cot_hbm, cot_ref))
    ):
        loads.append(pltpu.make_async_copy(src, dst, load_sem.at[i]))
        loads[-1].start()

    def send(src, dst, ssem, rsem, device):
        copy = pltpu.make_async_remote_copy(
            src_ref=src, dst_ref=dst, send_sem=ssem, recv_sem=rsem,
            device_id=device, device_id_type=MESH,
        )
        copy.start()
        return copy

    def zero_t(i, c):
        tmat[pl.ds(i * 16, 16), :] = jnp.zeros((16, 2048), BF)
        return c

    lax.fori_loop(0, 72, zero_t, 0)
    ef[...] = jnp.zeros((48, 128), F32)
    for ab in range(9):
        base = ab * 128
        for c in range(3):
            tap = fk_ref[ab * 3 + c].astype(F32)
            ef[16 + 4 * c : 20 + 4 * c, 0:64] = tap
            ef[20 + 4 * c : 24 + 4 * c, 64:128] = tap
        tiles = [ef[o : o + 16, :].astype(BF) for o in (4, 20, 12, 28)]
        for m in range(8):
            lo = slice(2 * m * 128, 2 * m * 128 + 128)
            hi = slice(2 * m * 128 + 128, 2 * m * 128 + 256)
            if m > 0:
                tmat[base + 16 * (m - 1) : base + 16 * m, lo] = tiles[0]
            tmat[base + 16 * m : base + 16 * m + 16, lo] = tiles[1]
            tmat[base + 16 * m : base + 16 * m + 16, hi] = tiles[2]
            if m < 7:
                tmat[base + 16 * (m + 1) : base + 16 * (m + 2), hi] = tiles[3]

    loads[0].wait()
    pl.semaphore_wait(barrier, NS - 1 + NQ - 1 + 1)

    v_down = send(vol_ref.at[0:2], vhalo.at[1], halo_send.at[0], halo_recv.at[0], {"space": down})
    v_up = send(vol_ref.at[2:4], vhalo.at[0], halo_send.at[1], halo_recv.at[1], {"space": up})

    loads[1].wait()
    for ab in range(9):
        k0 = km_ref[(ab * 3) * 64 : (ab * 3 + 1) * 64, :]
        k1 = km_ref[(ab * 3 + 1) * 64 : (ab * 3 + 2) * 64, :]
        k2 = km_ref[(ab * 3 + 2) * 64 : (ab * 3 + 3) * 64, :]
        z = jnp.zeros((64, 128), BF)
        base = ab * 256
        wmid[base : base + 64, 0:128] = k1
        wmid[base : base + 64, 128:256] = k0
        wmid[base + 64 : base + 128, 0:128] = k2
        wmid[base + 64 : base + 128, 128:256] = k1
        wmid[base + 128 : base + 192, 0:128] = z
        wmid[base + 128 : base + 192, 128:256] = k2
        wmid[base + 192 : base + 256, 0:128] = k0
        wmid[base + 192 : base + 256, 128:256] = z
    for i in range(6):
        xpad[i, 0:16, :] = jnp.zeros((16, 256), BF)
        xpad[i, 528:544, :] = jnp.zeros((16, 256), BF)
    for i in range(4):
        pcat[i, 0:16, :] = jnp.zeros((16, 384), BF)
        pcat[i, 272:288, :] = jnp.zeros((16, 384), BF)
    for i in range(2):
        gcat[i, 0:16, :] = jnp.zeros((16, 768), BF)
        gcat[i, 272:288, :] = jnp.zeros((16, 768), BF)
    mbuf[27 * 64 : 28 * 64, :] = jnp.zeros((64, 128), BF)

    def put_volume(row, value):
        rows = value.shape[0]
        edge = lax.broadcasted_iota(jnp.int32, (rows, 128), 0) % 32
        vf[8 : 8 + rows, :] = value
        volb[0, row : row + rows, :] = jnp.where(edge == 0, 0.0, vf[7 : 7 + rows, :]).astype(BF)
        volb[1, row : row + rows, :] = value.astype(BF)
        volb[2, row : row + rows, :] = jnp.where(edge == 31, 0.0, vf[9 : 9 + rows, :]).astype(BF)

    vf[0:8, :] = jnp.zeros((8, 128), F32)
    vf[136:144, :] = jnp.zeros((8, 128), F32)
    put_volume(64, vol_ref[...].astype(F32).reshape(128, 128))

    def first(plane):
        def step(m, c):
            lhs = jnp.concatenate(
                [
                    volb[b, 32 * (plane + a) : 32 * (plane + a) + 64, :]
                    for a in range(3)
                    for b in range(3)
                ],
                axis=1,
            )
            col = pl.multiple_of(m * 256, 256)
            ybuf[32 * plane : 32 * plane + 64, pl.ds(col, 256)] = act(
                dot(lhs, tmat[:, pl.ds(col, 256)])
            )
            return c

        lax.fori_loop(0, 8, step, 0)

    lane = lax.broadcasted_iota(jnp.int32, (32, 128), 1)
    zero = jnp.zeros((32, 128), F32)

    def put_hidden(i):
        ys = [ybuf[32 * i : 32 * i + 32, 128 * j : 128 * j + 128] for j in range(16)]
        for j in range(16):
            after = ys[j + 1] if j < 15 else zero
            before = ys[j - 1] if j > 0 else zero
            yst[0, pl.ds(j, 32, stride=16), :] = ys[j]
            yst[1, pl.ds(j, 32, stride=16), :] = jnp.where(lane < 64, after, before)
        xpad[i, 16:528, 0:128] = yst[0].astype(BF)
        xpad[i, 16:528, 128:256] = yst[1].astype(BF)

    first(2)
    put_hidden(2)
    put_hidden(3)

    v_up.wait()
    put_volume(0, jnp.where(s == 0, 0.0, vhalo[0].astype(F32)).reshape(64, 128))
    first(0)
    ybuf[0:32, :] = jnp.where(s == 0, 0.0, ybuf[0:32, :])
    put_hidden(0)
    put_hidden(1)

    prow = lax.broadcasted_iota(jnp.int32, (256, 128), 0) % 16
    pf[0:8, :] = jnp.zeros((8, 256), F32)
    pf[264:272, :] = jnp.zeros((8, 256), F32)

    def put_pooled(i, value):
        pf[8:264, 0:128] = value
        pcat[i, 16:272, 0:128] = jnp.where(prow == 0, 0.0, pf[7:263, 0:128]).astype(BF)
        pcat[i, 16:272, 128:256] = value.astype(BF)
        pcat[i, 16:272, 256:384] = jnp.where(prow == 15, 0.0, pf[9:265, 0:128]).astype(BF)

    def mid_plane(i):
        lhs = jnp.concatenate(
            [xpad[i + a, 16 * b : 16 * b + 512, :] for a in range(3) for b in range(3)], axis=1
        )
        pre = dot(lhs, wmid[...])
        pre_mid[i] = pre
        value = act(pre).reshape(16, 2, 16, 256)
        value = value[:, 0] + value[:, 1]
        return (value[:, :, :128] + value[:, :, 128:]).reshape(256, 128)

    p_copies = []

    def pool(plane):
        pooled = ((mid_plane(2 * plane) + mid_plane(2 * plane + 1)) * 0.125).astype(BF)
        pooled_send[plane] = pooled
        p_copies.append(
            send(
                pooled_send.at[plane], phalo.at[1 - plane], halo_send.at[2 + plane],
                halo_recv.at[2 + plane], {"space": down if plane == 0 else up},
            )
        )
        put_pooled(plane + 1, pooled.astype(F32))

    pool(0)

    v_down.wait()
    put_volume(192, jnp.where(s == NS - 1, 0.0, vhalo[1].astype(F32)).reshape(64, 128))
    first(4)
    ybuf[160:192, :] = jnp.where(s == NS - 1, 0.0, ybuf[160:192, :])
    put_hidden(4)
    put_hidden(5)
    pool(1)

    loads[2].wait()

    def deep_taps(plane, a):
        lhs = jnp.concatenate(
            [pcat[plane + a, 16 * b : 16 * b + 256, :] for b in range(3)], axis=1
        )
        return dot(lhs, kd_ref[a * 1152 : (a + 1) * 1152, :])

    predeep[0] = deep_taps(0, 1) + deep_taps(0, 2)
    predeep[1] = deep_taps(1, 0) + deep_taps(1, 1)

    for b in range(3):
        for i in range(6):
            xt[b * 256 : (b + 1) * 256, i * 512 : (i + 1) * 512] = xpad[i, 16 * b : 16 * b + 512, :].T

    def slopes(i, c):
        slope_mid[i] = 0.125 * act_slope(pre_mid[i])
        return c

    lax.fori_loop(0, 4, slopes, 0)

    def put_turned(i):
        for b in range(3):
            pt[b * 384 : (b + 1) * 384, i * 256 : (i + 1) * 256] = pcat[i, 16 * b : 16 * b + 256, :].T

    put_turned(1)
    put_turned(2)
    loads[3].wait()

    grow = lax.broadcasted_iota(jnp.int32, (256, 256), 0) % 16

    def put_grad(i, value):
        pf[8:264, :] = value
        gcat[i, 16:272, 0:256] = jnp.where(grow == 15, 0.0, pf[9:265, :]).astype(BF)
        gcat[i, 16:272, 256:512] = value.astype(BF)
        gcat[i, 16:272, 512:768] = jnp.where(grow == 0, 0.0, pf[7:263, :]).astype(BF)

    def back_taps(plane, a):
        total = None
        for b in range(3):
            for c in range(3):
                rows = 16 * (2 - b)
                tap = (a * 3 + b) * 3 + c
                term = dot(
                    gcat[plane, rows : rows + 256, 256 * c : 256 * c + 256],
                    kd_ref[tap * 128 : (tap + 1) * 128, :],
                    ((1,), (1,)),
                )
                total = term if total is None else total + term
        return total

    b_copies = []
    for plane in (1, 0):
        p_copies[1 - plane].wait()
        if plane == 1:
            put_pooled(3, jnp.where(s == NS - 1, 0.0, phalo[1].astype(F32)))
        else:
            put_pooled(0, jnp.where(s == 0, 0.0, phalo[0].astype(F32)))
        pre = predeep[plane] + deep_taps(plane, 0 if plane == 0 else 2)
        predeep[plane] = pre
        value = (cot_ref[plane].astype(F32) * act_slope(pre)).astype(BF)
        grad[plane] = value
        put_grad(plane, value.astype(F32))
        bsend[plane] = back_taps(plane, 0 if plane == 0 else 2).astype(BF)
        b_copies.append(
            send(
                bsend.at[plane], bhalo.at[1 - plane], halo_send.at[4 + plane],
                halo_recv.at[4 + plane], {"space": down if plane == 0 else up},
            )
        )

    put_turned(0)
    put_turned(3)
    gown = grad[...].reshape(512, 256)
    for a in range(3):
        term = dot(pt[:, a * 256 : a * 256 + 512], gown).astype(BF).reshape(9, 128, 256)
        dbuf[0, 9 * a : 9 * a + 9] = term[:, :, :128]
        dbuf[1, 9 * a : 9 * a + 9] = term[:, :, 128:]
    d_pair = send(dbuf.at[1 - core], drecv1, pair_send.at[0], pair_recv.at[0], {"dp": other})

    back = [back_taps(0, 1) + back_taps(1, 0), back_taps(1, 1) + back_taps(0, 2)]

    d_pair.wait()
    dsum1[...] = (dbuf[core].astype(F32) + drecv1[...].astype(F32)).astype(BF)
    d_space = []
    for k in range(1, NS):
        row = pl.multiple_of(space_peer(k) * CS, CS)
        d_space.append(
            send(
                dsum1.at[:, pl.ds(row, CS), :], drecv2.at[k], ds_send.at[k], ds_recv.at[k],
                {"space": space_peer(k)},
            )
        )

    out_ref[...] = act(predeep[...]).astype(BF)

    for plane in (1, 0):
        b_copies[plane].wait()
        edge = s == (0 if plane == 0 else NS - 1)
        total = back[plane] + jnp.where(edge, 0.0, bhalo[plane].astype(F32))
        total = total.astype(BF).astype(F32)
        wide = jnp.concatenate([total, total], axis=1).reshape(16, 1, 16, 256)
        for i in range(2):
            value = slope_mid[2 * plane + i].reshape(16, 2, 16, 256) * wide
            row = (2 * plane + i) * 512
            gmid[row : row + 512, :] = value.reshape(512, 256).astype(BF)

    def mid_grad(a):
        part = dot(xt[:, a * 512 : a * 512 + 2048], gmid[...])
        for b in range(3):
            r = part[b * 256 : (b + 1) * 256]
            row = (a * 3 + b) * 192
            mbuf[row : row + 64, :] = (r[0:64, 128:] + r[192:256, :128]).astype(BF)
            mbuf[row + 64 : row + 128, :] = (r[0:64, :128] + r[64:128, 128:]).astype(BF)
            mbuf[row + 128 : row + 192, :] = (r[64:128, :128] + r[128:192, 128:]).astype(BF)

    def m_pair(p):
        base, rows = MPARTS[p]
        half = rows // 2
        theirs = pl.multiple_of(base + (1 - core) * half, 16)
        return send(
            mbuf.at[pl.ds(theirs, half), :], mrecv1.at[base // 2 : base // 2 + half, :],
            mp_send.at[p], mp_recv.at[p], {"dp": other},
        )

    def m_space(p, pair):
        base, rows = MPARTS[p]
        half, one = rows // 2, rows // 2 // NS
        lo = base // 2
        pair.wait()
        mine = pl.multiple_of(base + core * half, 16)
        msum1[lo : lo + half, :] = (
            mbuf[pl.ds(mine, half), :].astype(F32) + mrecv1[lo : lo + half, :].astype(F32)
        ).astype(BF)
        copies = []
        for k in range(1, NS):
            row = pl.multiple_of(lo + space_peer(k) * one, 16)
            copies.append(
                send(
                    msum1.at[pl.ds(row, one), :], mrecv2.at[k, lo // NS : lo // NS + one, :],
                    ms_send.at[p, k], ms_recv.at[p, k], {"space": space_peer(k)},
                )
            )
        return copies

    def m_dp(p, copies):
        base, rows = MPARTS[p]
        one = rows // 2 // NS
        lo = base // 2
        for copy in copies:
            copy.wait()
        row = pl.multiple_of(lo + s * one, 16)
        total = msum1[pl.ds(row, one), :].astype(F32)
        for k in range(1, NS):
            total = total + mrecv2[k, lo // NS : lo // NS + one, :].astype(F32)
        part = mrecv3.at[q, lo // NS : lo // NS + one, :]
        part[...] = total.astype(BF)
        return [
            send(part, part, mq_send.at[p, k], mq_recv.at[p, k], {"dp": dp_peer(k)})
            for k in range(1, NQ)
        ]

    def m_gather(p, copies):
        base, rows = MPARTS[p]
        one = rows // 2 // NS
        lo = base // 2
        for copy in copies:
            copy.wait()
        total = mrecv3[0, lo // NS : lo // NS + one, :].astype(F32)
        for k in range(1, NQ):
            total = total + mrecv3[k, lo // NS : lo // NS + one, :].astype(F32)
        row = pl.multiple_of(lo + s * one, 16)
        mfull[pl.ds(row, one), :] = total.astype(BF)
        part = mfull.at[pl.ds(row, one), :]
        return [
            send(part, part, mg_send.at[p, k], mg_recv.at[p, k], {"space": space_peer(k)})
            for k in range(1, NS)
        ]

    def m_last(p, copies):
        base, rows = MPARTS[p]
        half = rows // 2
        lo = base // 2
        for copy in copies:
            copy.wait()
        copy = send(
            mfull.at[lo : lo + half, :], mout.at[lo : lo + half, :], mo_send.at[p], mo_recv.at[p],
            {"dp": other},
        )
        mk_ref[pl.ds(pl.multiple_of(base + core * half, 16), half), :] = mfull[lo : lo + half, :]
        return copy

    def m_store(p, copy):
        base, rows = MPARTS[p]
        half = rows // 2
        lo = base // 2
        copy.wait()
        theirs = pl.multiple_of(base + (1 - core) * half, 16)
        mk_ref[pl.ds(theirs, half), :] = mout[lo : lo + half, :]

    mid_grad(0)
    m0 = m_pair(0)
    mid_grad(1)
    m1 = m_pair(1)
    m0 = m_space(0, m0)
    mid_grad(2)
    m2 = m_pair(2)
    m1 = m_space(1, m1)
    m2 = m_space(2, m2)

    m0 = m_dp(0, m0)
    m1 = m_dp(1, m1)

    for copy in d_space:
        copy.wait()
    own_row = pl.multiple_of(s * CS, CS)
    total = dsum1[:, pl.ds(own_row, CS), :].astype(F32)
    for k in range(1, NS):
        total = total + drecv2[k].astype(F32)
    dsum2[0:DROWS, :] = total.reshape(DROWS, 128).astype(BF)
    dsum2[DROWS : NQ * DPIECE, :] = jnp.zeros((NQ * DPIECE - DROWS, 128), BF)
    d_dp = []
    for k in range(1, NQ):
        row = pl.multiple_of(lax.rem(q + k, NQ) * DPIECE, DPIECE)
        d_dp.append(
            send(
                dsum2.at[pl.ds(row, DPIECE), :], drecv3.at[k], dq_send.at[k], dq_recv.at[k],
                {"dp": dp_peer(k)},
            )
        )

    m2 = m_dp(2, m2)
    m0 = m_gather(0, m0)
    m1 = m_gather(1, m1)

    for copy in d_dp:
        copy.wait()
    q_row = pl.multiple_of(q * DPIECE, DPIECE)
    total = dsum2[pl.ds(q_row, DPIECE), :].astype(F32)
    for k in range(1, NQ):
        total = total + drecv3[k].astype(F32)
    dfull[pl.ds(q_row, DPIECE), :] = total.astype(BF)
    d_part = dfull.at[pl.ds(q_row, DPIECE), :]
    d_gather = [
        send(d_part, d_part, dg_send.at[k], dg_recv.at[k], {"dp": dp_peer(k)})
        for k in range(1, NQ)
    ]

    m2 = m_gather(2, m2)
    m0 = m_last(0, m0)
    m1 = m_last(1, m1)
    m_store(0, m0)
    m_store(1, m1)
    m2 = m_last(2, m2)
    for copy in d_gather:
        copy.wait()
    d_last = send(dfull, dother, pair_send.at[1], pair_recv.at[1], {"dp": other})
    m_store(2, m2)
    d_last.wait()
    mine = dfull[0:DROWS, :]
    theirs = dother[0:DROWS, :]
    dk_ref[:, 0:128] = jnp.where(core == 0, mine, theirs)
    dk_ref[:, 128:256] = jnp.where(core == 0, theirs, mine)


def finish(deep_ref, dk_ref, mk_ref, out_ref, dg_ref, mg_ref):
    deep_scale = math.sqrt(NQ * 2 * NS * 2 * 256)
    mid_scale = math.sqrt(NQ * 2 * NS * 4 * 1024)
    out_ref[...] = deep_ref[...]
    dg_ref[...] = dk_ref[...].astype(F32) * (1.0 / deep_scale)
    mg_ref[...] = mk_ref[0 : 27 * 64, :].astype(F32) * (1.0 / mid_scale)


def on_device(volume, first_kernel, mid_kernel, deep_kernel, deep_cotangent):
    vm = pl.BlockSpec(memory_space=pltpu.VMEM)
    hbm = pl.BlockSpec(memory_space=pltpu.HBM)
    dma = pltpu.SemaphoreType.DMA
    deep_out, deep_grad, mid_grad = pl.pallas_call(
        kernel,
        out_shape=(
            jax.ShapeDtypeStruct((2, 256, 256), BF),
            jax.ShapeDtypeStruct((DROWS, 256), BF),
            jax.ShapeDtypeStruct((MROWS, 128), BF),
        ),
        in_specs=[vm] + [hbm] * 4,
        out_specs=(vm, vm, vm),
        scratch_shapes=[
            pltpu.VMEM((4, 32, 128), BF),
            pltpu.VMEM((27 * 64, 128), BF),
            pltpu.VMEM((27 * 128, 256), BF),
            pltpu.VMEM((2, 256, 256), BF),
            pltpu.VMEM((2, 2, 32, 128), BF),
            pltpu.VMEM((48, 128), F32),
            pltpu.VMEM((144, 128), F32),
            pltpu.VMEM((3, 256, 128), BF),
            pltpu.VMEM((1152, 2048), BF),
            pltpu.VMEM((192, 2048), F32),
            pltpu.VMEM((2, 512, 128), F32),
            pltpu.VMEM((2304, 256), BF),
            pltpu.VMEM((6, 544, 256), BF),
            pltpu.VMEM((768, 3072), BF),
            pltpu.VMEM((4, 512, 256), F32),
            pltpu.VMEM((4, 512, 256), F32),
            pltpu.VMEM((2, 256, 128), BF),
            pltpu.VMEM((272, 256), F32),
            pltpu.VMEM((4, 288, 384), BF),
            pltpu.VMEM((1152, 1024), BF),
            pltpu.VMEM((2, 256, 128), BF),
            pltpu.VMEM((2, 256, 256), F32),
            pltpu.VMEM((2, 256, 256), BF),
            pltpu.VMEM((2, 256, 128), BF),
            pltpu.VMEM((2, 256, 128), BF),
            pltpu.VMEM((2, 288, 768), BF),
            pltpu.VMEM((2, 27, 128, 128), BF),
            pltpu.VMEM((27, 128, 128), BF),
            pltpu.VMEM((27, 128, 128), BF),
            pltpu.VMEM((NS, 27, CS, 128), BF),
            pltpu.VMEM((NQ * DPIECE, 128), BF),
            pltpu.VMEM((NQ, DPIECE, 128), BF),
            pltpu.VMEM((NQ * DPIECE, 128), BF),
            pltpu.VMEM((NQ * DPIECE, 128), BF),
            pltpu.VMEM((2048, 256), BF),
            pltpu.VMEM((MROWS, 128), BF),
            pltpu.VMEM((MHALF, 128), BF),
            pltpu.VMEM((MHALF, 128), BF),
            pltpu.VMEM((NS, MONE, 128), BF),
            pltpu.VMEM((NQ, MONE, 128), BF),
            pltpu.VMEM((MHALF, 128), BF),
            pltpu.VMEM((MHALF, 128), BF),
            dma((4,)), dma((6,)), dma((6,)), dma((2,)), dma((2,)),
            *[dma((8,)) for _ in range(6)],
            dma((3,)), dma((3,)),
            *[dma((3, 8)) for _ in range(6)],
            dma((3,)), dma((3,)),
        ],
        compiler_params=pltpu.CompilerParams(
            collective_id=0, has_side_effects=True, vmem_limit_bytes=44 * 1024 * 1024
        ),
    )(
        first_kernel.reshape(27, 4, 64),
        volume[0],
        mid_kernel.reshape(27 * 64, 128),
        deep_kernel.reshape(27 * 128, 256),
        deep_cotangent.reshape(2, 256, 256),
    )
    deep_out, deep_grad, mid_grad = pl.pallas_call(
        finish,
        out_shape=(
            jax.ShapeDtypeStruct((2, 256, 256), BF),
            jax.ShapeDtypeStruct((DROWS, 256), F32),
            jax.ShapeDtypeStruct((27 * 64, 128), F32),
        ),
        in_specs=[vm] * 3,
        out_specs=(vm, vm, vm),
        compiler_params=pltpu.CompilerParams(vmem_limit_bytes=8 * 1024 * 1024),
    )(deep_out, deep_grad, mid_grad)
    return (
        deep_out.reshape(1, 2, 16, 16, 256),
        deep_grad.reshape(3, 3, 3, CS, 256),
        mid_grad.reshape(3, 3, 3, 64, 128),
    )


def solution(mesh):
    in_specs = (P("dp", "space", None, None), P(), P(), P(), P("dp", "space", None, None, None))
    out_specs = (P("dp", "space", None, None, None), P(None, None, None, "space", None), P())
    return jax.shard_map(
        on_device, mesh=mesh, in_specs=in_specs, out_specs=out_specs, check_vma=False
    )
```

```python
import functools
import math

import jax
import jax.numpy as jnp
from jax import lax
from jax.experimental import pallas as pl
from jax.experimental.pallas import tpu as pltpu
from jax.sharding import PartitionSpec as P

SLOPE = 0.3
BF = jnp.bfloat16
F32 = jnp.float32
MESH = pl.DeviceIdType.MESH

NS = 8
NQ = 8
CS = 128 // NS
DROWS = 27 * CS
DPIECE = 64
DQUARTER = 28 * 32
MROWS = 28 * 64
MHALF = MROWS // 2
MPARTS = ((0, 512), (512, 512), (1024, 768))
MONE = MHALF // NS


def sigmoid(z):
    return 0.5 * jnp.tanh(0.5 * z) + 0.5


def act(z):
    return z * (SLOPE + (1.0 - SLOPE) * sigmoid(z))


def act_slope(z):
    s = sigmoid(z)
    return SLOPE + (1.0 - SLOPE) * (s + z * s * (1.0 - s))


def dot(a, b, dims=((1,), (0,))):
    return lax.dot_general(a, b, (dims, ((), ())), preferred_element_type=F32)


def kernel(
    fk_ref, vol_hbm, km_hbm, kd_hbm, cot_hbm,
    out_ref, dk_ref, mk_ref,
    vol_ref, km_ref, kd_ref, cot_ref,
    vhalo, ef, vf, volb, tmat, ybuf, yst, wmid, xpad, xt, pre_mid, slope_mid,
    phalo, pf, pcat, pt, pooled_send, predeep, grad, bsend, bhalo, gcat, dbuf, drecv1, dsum1,
    drecv2, dsum2, drecv3, dfull, dother, gmid, mbuf, mrecv1, msum1, mrecv2,
    mrecv3, mfull, mout,
    load_sem, halo_send, halo_recv, pair_send, pair_recv, ds_send, ds_recv, dq_send, dq_recv,
    dg_send, dg_recv, mp_send, mp_recv, ms_send, ms_recv, mq_send, mq_recv, mg_send, mg_recv,
    mo_send, mo_recv,
):
    s = lax.axis_index("space")
    d = lax.axis_index("dp")
    q = d // 2
    core = d % 2
    other = d + 1 - 2 * core

    def space_peer(k):
        return lax.rem(s + k, NS)

    def dp_peer(k):
        return lax.rem(q + k, NQ) * 2 + core

    first_core = core == 0
    y_low = s % 2
    z_chip = s // 2
    x_chip = q % 4
    y_high = q // 4
    ring = jnp.where(first_core, z_chip, x_chip)

    def ring_peer(k):
        place = lax.rem(ring + k, 4)
        return place, {
            "dp": jnp.where(first_core, d, (y_high * 4 + place) * 2 + core),
            "space": jnp.where(first_core, place * 2 + y_low, s),
        }

    def plane_peer(k):
        a = jnp.where(first_core, lax.rem(y_low + k // 8, 2), lax.rem(s + k // 2, 8))
        b = jnp.where(first_core, lax.rem(q + k % 8, 8), lax.rem(y_high + k % 2, 2))
        return jnp.where(first_core, a * 8 + b, a * 2 + b), {
            "dp": jnp.where(first_core, b, b * 4 + x_chip) * 2 + core,
            "space": jnp.where(first_core, z_chip * 2 + a, a),
        }

    up = space_peer(1)
    down = space_peer(NS - 1)

    barrier = pltpu.get_barrier_semaphore()
    for k in range(1, 16):
        pl.semaphore_signal(barrier, inc=1, device_id=plane_peer(k)[1], device_id_type=MESH)
    for k in range(6):
        place = lax.rem(ring + 1 + k // 2, 4)
        device = {
            "dp": jnp.where(first_core, d, ((k % 2) * 4 + place) * 2 + core),
            "space": jnp.where(first_core, place * 2 + k % 2, s),
        }
        pl.semaphore_signal(barrier, inc=1, device_id=device, device_id_type=MESH)
    pl.semaphore_signal(barrier, inc=1, device_id={"dp": other}, device_id_type=MESH)

    loads = []
    for i, (src, dst) in enumerate(
        ((vol_hbm, vol_ref), (km_hbm, km_ref), (kd_hbm, kd_ref), (cot_hbm, cot_ref))
    ):
        loads.append(pltpu.make_async_copy(src, dst, load_sem.at[i]))
        loads[-1].start()

    def send(src, dst, ssem, rsem, device):
        copy = pltpu.make_async_remote_copy(
            src_ref=src, dst_ref=dst, send_sem=ssem, recv_sem=rsem,
            device_id=device, device_id_type=MESH,
        )
        copy.start()
        return copy

    def zero_t(i, c):
        tmat[pl.ds(i * 16, 16), :] = jnp.zeros((16, 2048), BF)
        return c

    lax.fori_loop(0, 72, zero_t, 0)
    ef[...] = jnp.zeros((48, 128), F32)
    for ab in range(9):
        base = ab * 128
        for c in range(3):
            tap = fk_ref[ab * 3 + c].astype(F32)
            ef[16 + 4 * c : 20 + 4 * c, 0:64] = tap
            ef[20 + 4 * c : 24 + 4 * c, 64:128] = tap
        tiles = [ef[o : o + 16, :].astype(BF) for o in (4, 20, 12, 28)]
        for m in range(8):
            lo = slice(2 * m * 128, 2 * m * 128 + 128)
            hi = slice(2 * m * 128 + 128, 2 * m * 128 + 256)
            if m > 0:
                tmat[base + 16 * (m - 1) : base + 16 * m, lo] = tiles[0]
            tmat[base + 16 * m : base + 16 * m + 16, lo] = tiles[1]
            tmat[base + 16 * m : base + 16 * m + 16, hi] = tiles[2]
            if m < 7:
                tmat[base + 16 * (m + 1) : base + 16 * (m + 2), hi] = tiles[3]

    loads[0].wait()
    pl.semaphore_wait(barrier, 15 + 6 + 1)

    v_down = send(vol_ref.at[0:2], vhalo.at[1], halo_send.at[0], halo_recv.at[0], {"space": down})
    v_up = send(vol_ref.at[2:4], vhalo.at[0], halo_send.at[1], halo_recv.at[1], {"space": up})

    loads[1].wait()
    for ab in range(9):
        k0 = km_ref[(ab * 3) * 64 : (ab * 3 + 1) * 64, :]
        k1 = km_ref[(ab * 3 + 1) * 64 : (ab * 3 + 2) * 64, :]
        k2 = km_ref[(ab * 3 + 2) * 64 : (ab * 3 + 3) * 64, :]
        z = jnp.zeros((64, 128), BF)
        base = ab * 256
        wmid[base : base + 64, 0:128] = k1
        wmid[base : base + 64, 128:256] = k0
        wmid[base + 64 : base + 128, 0:128] = k2
        wmid[base + 64 : base + 128, 128:256] = k1
        wmid[base + 128 : base + 192, 0:128] = z
        wmid[base + 128 : base + 192, 128:256] = k2
        wmid[base + 192 : base + 256, 0:128] = k0
        wmid[base + 192 : base + 256, 128:256] = z
    for i in range(6):
        xpad[i, 0:16, :] = jnp.zeros((16, 256), BF)
        xpad[i, 528:544, :] = jnp.zeros((16, 256), BF)
    for i in range(4):
        pcat[i, 0:16, :] = jnp.zeros((16, 384), BF)
        pcat[i, 272:288, :] = jnp.zeros((16, 384), BF)
    for i in range(2):
        gcat[i, 0:16, :] = jnp.zeros((16, 768), BF)
        gcat[i, 272:288, :] = jnp.zeros((16, 768), BF)
    mbuf[27 * 64 : 28 * 64, :] = jnp.zeros((64, 128), BF)

    def put_volume(row, value):
        rows = value.shape[0]
        edge = lax.broadcasted_iota(jnp.int32, (rows, 128), 0) % 32
        vf[8 : 8 + rows, :] = value
        volb[0, row : row + rows, :] = jnp.where(edge == 0, 0.0, vf[7 : 7 + rows, :]).astype(BF)
        volb[1, row : row + rows, :] = value.astype(BF)
        volb[2, row : row + rows, :] = jnp.where(edge == 31, 0.0, vf[9 : 9 + rows, :]).astype(BF)

    vf[0:8, :] = jnp.zeros((8, 128), F32)
    vf[136:144, :] = jnp.zeros((8, 128), F32)
    put_volume(64, vol_ref[...].astype(F32).reshape(128, 128))

    def first(plane):
        def step(m, c):
            lhs = jnp.concatenate(
                [
                    volb[b, 32 * (plane + a) : 32 * (plane + a) + 64, :]
                    for a in range(3)
                    for b in range(3)
                ],
                axis=1,
            )
            col = pl.multiple_of(m * 256, 256)
            ybuf[32 * plane : 32 * plane + 64, pl.ds(col, 256)] = act(
                dot(lhs, tmat[:, pl.ds(col, 256)])
            )
            return c

        lax.fori_loop(0, 8, step, 0)

    lane = lax.broadcasted_iota(jnp.int32, (32, 128), 1)
    zero = jnp.zeros((32, 128), F32)

    def put_hidden(i):
        ys = [ybuf[32 * i : 32 * i + 32, 128 * j : 128 * j + 128] for j in range(16)]
        for j in range(16):
            after = ys[j + 1] if j < 15 else zero
            before = ys[j - 1] if j > 0 else zero
            yst[0, pl.ds(j, 32, stride=16), :] = ys[j]
            yst[1, pl.ds(j, 32, stride=16), :] = jnp.where(lane < 64, after, before)
        xpad[i, 16:528, 0:128] = yst[0].astype(BF)
        xpad[i, 16:528, 128:256] = yst[1].astype(BF)

    first(2)
    put_hidden(2)
    put_hidden(3)

    v_up.wait()
    put_volume(0, jnp.where(s == 0, 0.0, vhalo[0].astype(F32)).reshape(64, 128))
    first(0)
    ybuf[0:32, :] = jnp.where(s == 0, 0.0, ybuf[0:32, :])
    put_hidden(0)
    put_hidden(1)

    prow = lax.broadcasted_iota(jnp.int32, (256, 128), 0) % 16
    pf[0:8, :] = jnp.zeros((8, 256), F32)
    pf[264:272, :] = jnp.zeros((8, 256), F32)

    def put_pooled(i, value):
        pf[8:264, 0:128] = value
        pcat[i, 16:272, 0:128] = jnp.where(prow == 0, 0.0, pf[7:263, 0:128]).astype(BF)
        pcat[i, 16:272, 128:256] = value.astype(BF)
        pcat[i, 16:272, 256:384] = jnp.where(prow == 15, 0.0, pf[9:265, 0:128]).astype(BF)

    def mid_plane(i):
        lhs = jnp.concatenate(
            [xpad[i + a, 16 * b : 16 * b + 512, :] for a in range(3) for b in range(3)], axis=1
        )
        pre = dot(lhs, wmid[...])
        pre_mid[i] = pre
        value = act(pre).reshape(16, 2, 16, 256)
        value = value[:, 0] + value[:, 1]
        return (value[:, :, :128] + value[:, :, 128:]).reshape(256, 128)

    p_copies = []

    def pool(plane):
        pooled = ((mid_plane(2 * plane) + mid_plane(2 * plane + 1)) * 0.125).astype(BF)
        pooled_send[plane] = pooled
        p_copies.append(
            send(
                pooled_send.at[plane], phalo.at[1 - plane], halo_send.at[2 + plane],
                halo_recv.at[2 + plane], {"space": down if plane == 0 else up},
            )
        )
        put_pooled(plane + 1, pooled.astype(F32))

    pool(0)

    v_down.wait()
    put_volume(192, jnp.where(s == NS - 1, 0.0, vhalo[1].astype(F32)).reshape(64, 128))
    first(4)
    ybuf[160:192, :] = jnp.where(s == NS - 1, 0.0, ybuf[160:192, :])
    put_hidden(4)
    put_hidden(5)
    pool(1)

    loads[2].wait()

    def deep_taps(plane, a):
        lhs = jnp.concatenate(
            [pcat[plane + a, 16 * b : 16 * b + 256, :] for b in range(3)], axis=1
        )
        return dot(lhs, kd_ref[a * 1152 : (a + 1) * 1152, :])

    predeep[0] = deep_taps(0, 1) + deep_taps(0, 2)
    predeep[1] = deep_taps(1, 0) + deep_taps(1, 1)

    for b in range(3):
        for i in range(6):
            xt[b * 256 : (b + 1) * 256, i * 512 : (i + 1) * 512] = xpad[i, 16 * b : 16 * b + 512, :].T

    def slopes(i, c):
        slope_mid[i] = 0.125 * act_slope(pre_mid[i])
        return c

    lax.fori_loop(0, 4, slopes, 0)

    def put_turned(i):
        for b in range(3):
            pt[b * 384 : (b + 1) * 384, i * 256 : (i + 1) * 256] = pcat[i, 16 * b : 16 * b + 256, :].T

    put_turned(1)
    put_turned(2)
    loads[3].wait()

    grow = lax.broadcasted_iota(jnp.int32, (256, 256), 0) % 16

    def put_grad(i, value):
        pf[8:264, :] = value
        gcat[i, 16:272, 0:256] = jnp.where(grow == 15, 0.0, pf[9:265, :]).astype(BF)
        gcat[i, 16:272, 256:512] = value.astype(BF)
        gcat[i, 16:272, 512:768] = jnp.where(grow == 0, 0.0, pf[7:263, :]).astype(BF)

    def back_taps(plane, a):
        total = None
        for b in range(3):
            for c in range(3):
                rows = 16 * (2 - b)
                tap = (a * 3 + b) * 3 + c
                term = dot(
                    gcat[plane, rows : rows + 256, 256 * c : 256 * c + 256],
                    kd_ref[tap * 128 : (tap + 1) * 128, :],
                    ((1,), (1,)),
                )
                total = term if total is None else total + term
        return total

    b_copies = []
    for plane in (1, 0):
        p_copies[1 - plane].wait()
        if plane == 1:
            put_pooled(3, jnp.where(s == NS - 1, 0.0, phalo[1].astype(F32)))
        else:
            put_pooled(0, jnp.where(s == 0, 0.0, phalo[0].astype(F32)))
        pre = predeep[plane] + deep_taps(plane, 0 if plane == 0 else 2)
        predeep[plane] = pre
        value = (cot_ref[plane].astype(F32) * act_slope(pre)).astype(BF)
        grad[plane] = value
        put_grad(plane, value.astype(F32))
        bsend[plane] = back_taps(plane, 0 if plane == 0 else 2).astype(BF)
        b_copies.append(
            send(
                bsend.at[plane], bhalo.at[1 - plane], halo_send.at[4 + plane],
                halo_recv.at[4 + plane], {"space": down if plane == 0 else up},
            )
        )

    put_turned(0)
    put_turned(3)
    gown = grad[...].reshape(512, 256)
    for a in range(3):
        term = dot(pt[:, a * 256 : a * 256 + 512], gown).astype(BF).reshape(9, 128, 256)
        dbuf[0, 9 * a : 9 * a + 9] = term[:, :, :128]
        dbuf[1, 9 * a : 9 * a + 9] = term[:, :, 128:]
    d_pair = send(dbuf.at[1 - core], drecv1, pair_send.at[0], pair_recv.at[0], {"dp": other})

    back = [back_taps(0, 1) + back_taps(1, 0), back_taps(1, 1) + back_taps(0, 2)]

    d_pair.wait()
    dsum = (dbuf[core].astype(F32) + drecv1[...].astype(F32)).astype(BF)

    @pl.when(first_core)
    def _():
        for place in range(4):
            dsum1[place, 0:864, :] = dsum[:, 32 * place : 32 * place + 32, :].reshape(864, 128)
            dsum1[place, 864:896, :] = jnp.zeros((32, 128), BF)

    @pl.when(jnp.logical_not(first_core))
    def _():
        for place in range(4):
            taps = 7 if place < 3 else 6
            dsum1[place, 0 : taps * 128, :] = dsum[7 * place : 7 * place + taps].reshape(taps * 128, 128)
        dsum1[3, 768:896, :] = jnp.zeros((128, 128), BF)

    d_ring = []
    for k in range(1, 4):
        place, device = ring_peer(k)
        d_ring.append(send(dsum1.at[place], drecv2.at[k], ds_send.at[k], ds_recv.at[k], device))

    out_ref[...] = act(predeep[...]).astype(BF)

    for plane in (1, 0):
        b_copies[plane].wait()
        edge = s == (0 if plane == 0 else NS - 1)
        total = back[plane] + jnp.where(edge, 0.0, bhalo[plane].astype(F32))
        total = total.astype(BF).astype(F32)
        wide = jnp.concatenate([total, total], axis=1).reshape(16, 1, 16, 256)
        for i in range(2):
            value = slope_mid[2 * plane + i].reshape(16, 2, 16, 256) * wide
            row = (2 * plane + i) * 512
            gmid[row : row + 512, :] = value.reshape(512, 256).astype(BF)

    def mid_grad(a):
        part = dot(xt[:, a * 512 : a * 512 + 2048], gmid[...])
        for b in range(3):
            r = part[b * 256 : (b + 1) * 256]
            row = (a * 3 + b) * 192
            mbuf[row : row + 64, :] = (r[0:64, 128:] + r[192:256, :128]).astype(BF)
            mbuf[row + 64 : row + 128, :] = (r[0:64, :128] + r[64:128, 128:]).astype(BF)
            mbuf[row + 128 : row + 192, :] = (r[64:128, :128] + r[128:192, 128:]).astype(BF)

    def m_pair(p):
        base, rows = MPARTS[p]
        half = rows // 2
        theirs = pl.multiple_of(base + (1 - core) * half, 16)
        return send(
            mbuf.at[pl.ds(theirs, half), :], mrecv1.at[base // 2 : base // 2 + half, :],
            mp_send.at[p], mp_recv.at[p], {"dp": other},
        )

    def m_space(p, pair):
        base, rows = MPARTS[p]
        half, one = rows // 2, rows // 2 // NS
        lo = base // 2
        pair.wait()
        mine = pl.multiple_of(base + core * half, 16)
        msum1[lo : lo + half, :] = (
            mbuf[pl.ds(mine, half), :].astype(F32) + mrecv1[lo : lo + half, :].astype(F32)
        ).astype(BF)
        copies = []
        for k in range(1, NS):
            row = pl.multiple_of(lo + space_peer(k) * one, 16)
            copies.append(
                send(
                    msum1.at[pl.ds(row, one), :], mrecv2.at[k, lo // NS : lo // NS + one, :],
                    ms_send.at[p, k], ms_recv.at[p, k], {"space": space_peer(k)},
                )
            )
        return copies

    def m_dp(p, copies):
        base, rows = MPARTS[p]
        one = rows // 2 // NS
        lo = base // 2
        for copy in copies:
            copy.wait()
        row = pl.multiple_of(lo + s * one, 16)
        total = msum1[pl.ds(row, one), :].astype(F32)
        for k in range(1, NS):
            total = total + mrecv2[k, lo // NS : lo // NS + one, :].astype(F32)
        part = mrecv3.at[q, lo // NS : lo // NS + one, :]
        part[...] = total.astype(BF)
        return [
            send(part, part, mq_send.at[p, k], mq_recv.at[p, k], {"dp": dp_peer(k)})
            for k in range(1, NQ)
        ]

    def m_gather(p, copies):
        base, rows = MPARTS[p]
        one = rows // 2 // NS
        lo = base // 2
        for copy in copies:
            copy.wait()
        total = mrecv3[0, lo // NS : lo // NS + one, :].astype(F32)
        for k in range(1, NQ):
            total = total + mrecv3[k, lo // NS : lo // NS + one, :].astype(F32)
        row = pl.multiple_of(lo + s * one, 16)
        mfull[pl.ds(row, one), :] = total.astype(BF)
        part = mfull.at[pl.ds(row, one), :]
        return [
            send(part, part, mg_send.at[p, k], mg_recv.at[p, k], {"space": space_peer(k)})
            for k in range(1, NS)
        ]

    def m_last(p, copies):
        base, rows = MPARTS[p]
        half = rows // 2
        lo = base // 2
        for copy in copies:
            copy.wait()
        copy = send(
            mfull.at[lo : lo + half, :], mout.at[lo : lo + half, :], mo_send.at[p], mo_recv.at[p],
            {"dp": other},
        )
        mk_ref[pl.ds(pl.multiple_of(base + core * half, 16), half), :] = mfull[lo : lo + half, :]
        return copy

    def m_store(p, copy):
        base, rows = MPARTS[p]
        half = rows // 2
        lo = base // 2
        copy.wait()
        theirs = pl.multiple_of(base + (1 - core) * half, 16)
        mk_ref[pl.ds(theirs, half), :] = mout[lo : lo + half, :]

    mid_grad(0)
    m0 = m_pair(0)
    mid_grad(1)
    m1 = m_pair(1)
    m0 = m_space(0, m0)
    mid_grad(2)
    m2 = m_pair(2)
    m1 = m_space(1, m1)
    m2 = m_space(2, m2)

    m0 = m_dp(0, m0)
    m1 = m_dp(1, m1)

    for copy in d_ring:
        copy.wait()
    total = dsum1[ring].astype(F32)
    for k in range(1, 4):
        total = total + drecv2[k].astype(F32)
    total = total.astype(BF)

    @pl.when(first_core)
    def _():
        rows = total.reshape(28, 2, 16, 128)
        for a in range(2):
            for b in range(7):
                dsum2[a * 8 + b] = rows[4 * b : 4 * b + 4, a].reshape(64, 128)
            dsum2[a * 8 + 7] = jnp.zeros((64, 128), BF)

    @pl.when(jnp.logical_not(first_core))
    def _():
        rows = total.reshape(7, 8, 16, 128)
        for a in range(8):
            dsum2[a * 2] = rows[0:4, a].reshape(64, 128)
            dsum2[a * 2 + 1, 0:48, :] = rows[4:7, a].reshape(48, 128)
            dsum2[a * 2 + 1, 48:64, :] = jnp.zeros((16, 128), BF)

    d_plane = []
    for k in range(1, 16):
        place, device = plane_peer(k)
        d_plane.append(send(dsum2.at[place], drecv3.at[k], dq_send.at[k], dq_recv.at[k], device))

    m2 = m_dp(2, m2)
    m0 = m_gather(0, m0)
    m1 = m_gather(1, m1)

    for copy in d_plane:
        copy.wait()
    total = dsum2[plane_peer(0)[0]].astype(F32)
    for k in range(1, 16):
        total = total + drecv3[k].astype(F32)
    dfull[q] = total.astype(BF)
    d_gather = [
        send(dfull.at[q], dfull.at[q], dg_send.at[k], dg_recv.at[k], {"dp": dp_peer(k)})
        for k in range(1, NQ)
    ]

    m2 = m_gather(2, m2)
    m0 = m_last(0, m0)
    m1 = m_last(1, m1)
    m_store(0, m0)
    m_store(1, m1)
    m2 = m_last(2, m2)
    for copy in d_gather:
        copy.wait()
    d_last = send(dfull, dother, pair_send.at[1], pair_recv.at[1], {"dp": other})
    m_store(2, m2)
    d_last.wait()
    left = jnp.where(first_core, dfull[...], dother[...]).reshape(NQ * DPIECE, 128)
    dk_ref[:, 0:128] = left[0:DROWS]
    right = jnp.where(first_core, dother[...], dfull[...])
    for place in range(4):
        row = 7 * 16 * place
        dk_ref[row : row + 64, 128:256] = right[place]
        rest = 48 if place < 3 else 32
        dk_ref[row + 64 : row + 64 + rest, 128:256] = right[4 + place, 0:rest]


def finish(deep_ref, dk_ref, mk_ref, out_ref, dg_ref, mg_ref):
    deep_scale = math.sqrt(NQ * 2 * NS * 2 * 256)
    mid_scale = math.sqrt(NQ * 2 * NS * 4 * 1024)
    out_ref[...] = deep_ref[...]
    dg_ref[...] = dk_ref[...].astype(F32) * (1.0 / deep_scale)
    mg_ref[...] = mk_ref[0 : 27 * 64, :].astype(F32) * (1.0 / mid_scale)


def on_device(volume, first_kernel, mid_kernel, deep_kernel, deep_cotangent):
    vm = pl.BlockSpec(memory_space=pltpu.VMEM)
    hbm = pl.BlockSpec(memory_space=pltpu.HBM)
    dma = pltpu.SemaphoreType.DMA
    deep_out, deep_grad, mid_grad = pl.pallas_call(
        kernel,
        out_shape=(
            jax.ShapeDtypeStruct((2, 256, 256), BF),
            jax.ShapeDtypeStruct((DROWS, 256), BF),
            jax.ShapeDtypeStruct((MROWS, 128), BF),
        ),
        in_specs=[vm] + [hbm] * 4,
        out_specs=(vm, vm, vm),
        scratch_shapes=[
            pltpu.VMEM((4, 32, 128), BF),
            pltpu.VMEM((27 * 64, 128), BF),
            pltpu.VMEM((27 * 128, 256), BF),
            pltpu.VMEM((2, 256, 256), BF),
            pltpu.VMEM((2, 2, 32, 128), BF),
            pltpu.VMEM((48, 128), F32),
            pltpu.VMEM((144, 128), F32),
            pltpu.VMEM((3, 256, 128), BF),
            pltpu.VMEM((1152, 2048), BF),
            pltpu.VMEM((192, 2048), F32),
            pltpu.VMEM((2, 512, 128), F32),
            pltpu.VMEM((2304, 256), BF),
            pltpu.VMEM((6, 544, 256), BF),
            pltpu.VMEM((768, 3072), BF),
            pltpu.VMEM((4, 512, 256), F32),
            pltpu.VMEM((4, 512, 256), F32),
            pltpu.VMEM((2, 256, 128), BF),
            pltpu.VMEM((272, 256), F32),
            pltpu.VMEM((4, 288, 384), BF),
            pltpu.VMEM((1152, 1024), BF),
            pltpu.VMEM((2, 256, 128), BF),
            pltpu.VMEM((2, 256, 256), F32),
            pltpu.VMEM((2, 256, 256), BF),
            pltpu.VMEM((2, 256, 128), BF),
            pltpu.VMEM((2, 256, 128), BF),
            pltpu.VMEM((2, 288, 768), BF),
            pltpu.VMEM((2, 27, 128, 128), BF),
            pltpu.VMEM((27, 128, 128), BF),
            pltpu.VMEM((4, DQUARTER, 128), BF),
            pltpu.VMEM((4, DQUARTER, 128), BF),
            pltpu.VMEM((16, DPIECE, 128), BF),
            pltpu.VMEM((16, DPIECE, 128), BF),
            pltpu.VMEM((NQ, DPIECE, 128), BF),
            pltpu.VMEM((NQ, DPIECE, 128), BF),
            pltpu.VMEM((2048, 256), BF),
            pltpu.VMEM((MROWS, 128), BF),
            pltpu.VMEM((MHALF, 128), BF),
            pltpu.VMEM((MHALF, 128), BF),
            pltpu.VMEM((NS, MONE, 128), BF),
            pltpu.VMEM((NQ, MONE, 128), BF),
            pltpu.VMEM((MHALF, 128), BF),
            pltpu.VMEM((MHALF, 128), BF),
            dma((4,)), dma((6,)), dma((6,)), dma((2,)), dma((2,)),
            dma((4,)), dma((4,)), dma((16,)), dma((16,)), dma((8,)), dma((8,)),
            dma((3,)), dma((3,)),
            *[dma((3, 8)) for _ in range(6)],
            dma((3,)), dma((3,)),
        ],
        compiler_params=pltpu.CompilerParams(
            collective_id=0, has_side_effects=True, vmem_limit_bytes=44 * 1024 * 1024
        ),
    )(
        *[pltpu.with_memory_space_constraint(x, pltpu.HBM) for x in (first_kernel.reshape(27, 4, 64),
        volume[0],
        mid_kernel.reshape(27 * 64, 128),
        deep_kernel.reshape(27 * 128, 256),
        deep_cotangent.reshape(2, 256, 256))],
    )
    deep_out, deep_grad, mid_grad = pl.pallas_call(
        finish,
        out_shape=(
            jax.ShapeDtypeStruct((2, 256, 256), BF),
            jax.ShapeDtypeStruct((DROWS, 256), F32),
            jax.ShapeDtypeStruct((27 * 64, 128), F32),
        ),
        in_specs=[vm] * 3,
        out_specs=(vm, vm, vm),
        compiler_params=pltpu.CompilerParams(vmem_limit_bytes=8 * 1024 * 1024),
    )(deep_out, deep_grad, mid_grad)
    return (
        deep_out.reshape(1, 2, 16, 16, 256),
        deep_grad.reshape(3, 3, 3, CS, 256),
        mid_grad.reshape(3, 3, 3, 64, 128),
    )


def solution(mesh):
    in_specs = (P("dp", "space", None, None), P(), P(), P(), P("dp", "space", None, None, None))
    out_specs = (P("dp", "space", None, None, None), P(None, None, None, "space", None), P())
    return jax.shard_map(
        on_device, mesh=mesh, in_specs=in_specs, out_specs=out_specs, check_vma=False
    )
```

```python
import functools
import math

import jax
import jax.numpy as jnp
from jax import lax
from jax.experimental import pallas as pl
from jax.experimental.pallas import tpu as pltpu
from jax.sharding import PartitionSpec as P

SLOPE = 0.3
BF = jnp.bfloat16
F32 = jnp.float32
MESH = pl.DeviceIdType.MESH

NS = 8
NQ = 8
CS = 128 // NS
DROWS = 27 * CS
DPIECE = 64
DQUARTER = 28 * 32
MROWS = 28 * 64
MHALF = MROWS // 2
MPARTS = ((0, 512), (512, 512), (1024, 768))
MONE = MHALF // NS


def sigmoid(z):
    return 0.5 * jnp.tanh(0.5 * z) + 0.5


def act(z):
    return z * (SLOPE + (1.0 - SLOPE) * sigmoid(z))


def act_slope(z):
    s = sigmoid(z)
    return SLOPE + (1.0 - SLOPE) * (s + z * s * (1.0 - s))


def dot(a, b, dims=((1,), (0,))):
    return lax.dot_general(a, b, (dims, ((), ())), preferred_element_type=F32)


def kernel(
    fk_ref, vol_hbm, km_hbm, kd_hbm, cot_hbm,
    out_ref, dk_ref, mk_ref,
    vol_ref, km_ref, kd_ref, cot_ref,
    vhalo, ef, vf, volb, tmat, ybuf, yst, wmid, xpad, pre_mid, slope_mid,
    phalo, pf, pcat, pooled_send, predeep, grad, bsend, bhalo, gcat, dbuf, drecv1, dsum1,
    drecv2, dsum2, drecv3, dfull, dother, gmid, mbuf, mrecv1, msum1, mrecv2,
    mrecv3, mfull, mout,
    load_sem, halo_send, halo_recv, pair_send, pair_recv, ds_send, ds_recv, dq_send, dq_recv,
    dg_send, dg_recv, mp_send, mp_recv, ms_send, ms_recv, mq_send, mq_recv, mg_send, mg_recv,
    mo_send, mo_recv,
):
    s = lax.axis_index("space")
    d = lax.axis_index("dp")
    q = d // 2
    core = d % 2
    other = d + 1 - 2 * core

    def space_peer(k):
        return lax.rem(s + k, NS)

    def dp_peer(k):
        return lax.rem(q + k, NQ) * 2 + core

    first_core = core == 0
    y_low = s % 2
    z_chip = s // 2
    x_chip = q % 4
    y_high = q // 4
    ring = jnp.where(first_core, z_chip, x_chip)

    def ring_peer(k):
        place = lax.rem(ring + k, 4)
        return place, {
            "dp": jnp.where(first_core, d, (y_high * 4 + place) * 2 + core),
            "space": jnp.where(first_core, place * 2 + y_low, s),
        }

    def plane_peer(k):
        a = jnp.where(first_core, lax.rem(y_low + k // 8, 2), lax.rem(s + k // 2, 8))
        b = jnp.where(first_core, lax.rem(q + k % 8, 8), lax.rem(y_high + k % 2, 2))
        return jnp.where(first_core, a * 8 + b, a * 2 + b), {
            "dp": jnp.where(first_core, b, b * 4 + x_chip) * 2 + core,
            "space": jnp.where(first_core, z_chip * 2 + a, a),
        }

    up = space_peer(1)
    down = space_peer(NS - 1)

    barrier = pltpu.get_barrier_semaphore()
    for k in range(1, 16):
        pl.semaphore_signal(barrier, inc=1, device_id=plane_peer(k)[1], device_id_type=MESH)
    for k in range(6):
        place = lax.rem(ring + 1 + k // 2, 4)
        device = {
            "dp": jnp.where(first_core, d, ((k % 2) * 4 + place) * 2 + core),
            "space": jnp.where(first_core, place * 2 + k % 2, s),
        }
        pl.semaphore_signal(barrier, inc=1, device_id=device, device_id_type=MESH)
    pl.semaphore_signal(barrier, inc=1, device_id={"dp": other}, device_id_type=MESH)

    loads = []
    for i, (src, dst) in enumerate(
        ((vol_hbm, vol_ref), (km_hbm, km_ref), (kd_hbm, kd_ref), (cot_hbm, cot_ref))
    ):
        loads.append(pltpu.make_async_copy(src, dst, load_sem.at[i]))
        loads[-1].start()

    def send(src, dst, ssem, rsem, device):
        copy = pltpu.make_async_remote_copy(
            src_ref=src, dst_ref=dst, send_sem=ssem, recv_sem=rsem,
            device_id=device, device_id_type=MESH,
        )
        copy.start()
        return copy

    def zero_t(i, c):
        tmat[pl.ds(i * 16, 16), :] = jnp.zeros((16, 2048), BF)
        return c

    lax.fori_loop(0, 72, zero_t, 0)
    ef[...] = jnp.zeros((48, 128), F32)
    for ab in range(9):
        base = ab * 128
        for c in range(3):
            tap = fk_ref[ab * 3 + c].astype(F32)
            ef[16 + 4 * c : 20 + 4 * c, 0:64] = tap
            ef[20 + 4 * c : 24 + 4 * c, 64:128] = tap
        tiles = [ef[o : o + 16, :].astype(BF) for o in (4, 20, 12, 28)]
        for m in range(8):
            lo = slice(2 * m * 128, 2 * m * 128 + 128)
            hi = slice(2 * m * 128 + 128, 2 * m * 128 + 256)
            if m > 0:
                tmat[base + 16 * (m - 1) : base + 16 * m, lo] = tiles[0]
            tmat[base + 16 * m : base + 16 * m + 16, lo] = tiles[1]
            tmat[base + 16 * m : base + 16 * m + 16, hi] = tiles[2]
            if m < 7:
                tmat[base + 16 * (m + 1) : base + 16 * (m + 2), hi] = tiles[3]

    loads[0].wait()
    pl.semaphore_wait(barrier, 15 + 6 + 1)

    v_down = send(vol_ref.at[0:2], vhalo.at[1], halo_send.at[0], halo_recv.at[0], {"space": down})
    v_up = send(vol_ref.at[2:4], vhalo.at[0], halo_send.at[1], halo_recv.at[1], {"space": up})

    loads[1].wait()
    for ab in range(9):
        k0 = km_ref[(ab * 3) * 64 : (ab * 3 + 1) * 64, :]
        k1 = km_ref[(ab * 3 + 1) * 64 : (ab * 3 + 2) * 64, :]
        k2 = km_ref[(ab * 3 + 2) * 64 : (ab * 3 + 3) * 64, :]
        z = jnp.zeros((64, 128), BF)
        base = ab * 256
        wmid[base : base + 64, 0:128] = k1
        wmid[base : base + 64, 128:256] = k0
        wmid[base + 64 : base + 128, 0:128] = k2
        wmid[base + 64 : base + 128, 128:256] = k1
        wmid[base + 128 : base + 192, 0:128] = z
        wmid[base + 128 : base + 192, 128:256] = k2
        wmid[base + 192 : base + 256, 0:128] = k0
        wmid[base + 192 : base + 256, 128:256] = z
    for i in range(6):
        xpad[i, 0:16, :] = jnp.zeros((16, 256), BF)
        xpad[i, 528:544, :] = jnp.zeros((16, 256), BF)
    for i in range(4):
        pcat[i, 0:16, :] = jnp.zeros((16, 384), BF)
        pcat[i, 272:288, :] = jnp.zeros((16, 384), BF)
    for i in range(2):
        gcat[i, 0:16, :] = jnp.zeros((16, 768), BF)
        gcat[i, 272:288, :] = jnp.zeros((16, 768), BF)
    mbuf[27 * 64 : 28 * 64, :] = jnp.zeros((64, 128), BF)

    def put_volume(row, value):
        rows = value.shape[0]
        edge = lax.broadcasted_iota(jnp.int32, (rows, 128), 0) % 32
        vf[8 : 8 + rows, :] = value
        volb[0, row : row + rows, :] = jnp.where(edge == 0, 0.0, vf[7 : 7 + rows, :]).astype(BF)
        volb[1, row : row + rows, :] = value.astype(BF)
        volb[2, row : row + rows, :] = jnp.where(edge == 31, 0.0, vf[9 : 9 + rows, :]).astype(BF)

    vf[0:8, :] = jnp.zeros((8, 128), F32)
    vf[136:144, :] = jnp.zeros((8, 128), F32)
    put_volume(64, vol_ref[...].astype(F32).reshape(128, 128))

    def first(plane):
        def step(m, c):
            lhs = jnp.concatenate(
                [
                    volb[b, 32 * (plane + a) : 32 * (plane + a) + 64, :]
                    for a in range(3)
                    for b in range(3)
                ],
                axis=1,
            )
            col = pl.multiple_of(m * 256, 256)
            ybuf[32 * plane : 32 * plane + 64, pl.ds(col, 256)] = act(
                dot(lhs, tmat[:, pl.ds(col, 256)])
            )
            return c

        lax.fori_loop(0, 8, step, 0)

    lane = lax.broadcasted_iota(jnp.int32, (32, 128), 1)
    zero = jnp.zeros((32, 128), F32)

    def put_hidden(i):
        ys = [ybuf[32 * i : 32 * i + 32, 128 * j : 128 * j + 128] for j in range(16)]
        for j in range(16):
            after = ys[j + 1] if j < 15 else zero
            before = ys[j - 1] if j > 0 else zero
            yst[0, pl.ds(j, 32, stride=16), :] = ys[j]
            yst[1, pl.ds(j, 32, stride=16), :] = jnp.where(lane < 64, after, before)
        xpad[i, 16:528, 0:128] = yst[0].astype(BF)
        xpad[i, 16:528, 128:256] = yst[1].astype(BF)

    first(2)
    put_hidden(2)
    put_hidden(3)

    v_up.wait()
    put_volume(0, jnp.where(s == 0, 0.0, vhalo[0].astype(F32)).reshape(64, 128))
    first(0)
    ybuf[0:32, :] = jnp.where(s == 0, 0.0, ybuf[0:32, :])
    put_hidden(0)
    put_hidden(1)

    prow = lax.broadcasted_iota(jnp.int32, (256, 128), 0) % 16
    pf[0:8, :] = jnp.zeros((8, 256), F32)
    pf[264:272, :] = jnp.zeros((8, 256), F32)

    def put_pooled(i, value):
        pf[8:264, 0:128] = value
        pcat[i, 16:272, 0:128] = jnp.where(prow == 0, 0.0, pf[7:263, 0:128]).astype(BF)
        pcat[i, 16:272, 128:256] = value.astype(BF)
        pcat[i, 16:272, 256:384] = jnp.where(prow == 15, 0.0, pf[9:265, 0:128]).astype(BF)

    def mid_plane(i):
        lhs = jnp.concatenate(
            [xpad[i + a, 16 * b : 16 * b + 512, :] for a in range(3) for b in range(3)], axis=1
        )
        pre = dot(lhs, wmid[...])
        pre_mid[i] = pre
        value = act(pre).reshape(16, 2, 16, 256)
        value = value[:, 0] + value[:, 1]
        return (value[:, :, :128] + value[:, :, 128:]).reshape(256, 128)

    p_copies = []

    def pool(plane):
        pooled = ((mid_plane(2 * plane) + mid_plane(2 * plane + 1)) * 0.125).astype(BF)
        pooled_send[plane] = pooled
        p_copies.append(
            send(
                pooled_send.at[plane], phalo.at[1 - plane], halo_send.at[2 + plane],
                halo_recv.at[2 + plane], {"space": down if plane == 0 else up},
            )
        )
        put_pooled(plane + 1, pooled.astype(F32))

    pool(0)

    v_down.wait()
    put_volume(192, jnp.where(s == NS - 1, 0.0, vhalo[1].astype(F32)).reshape(64, 128))
    first(4)
    ybuf[160:192, :] = jnp.where(s == NS - 1, 0.0, ybuf[160:192, :])
    put_hidden(4)
    put_hidden(5)
    pool(1)

    loads[2].wait()

    def deep_taps(plane, a):
        lhs = jnp.concatenate(
            [pcat[plane + a, 16 * b : 16 * b + 256, :] for b in range(3)], axis=1
        )
        return dot(lhs, kd_ref[a * 1152 : (a + 1) * 1152, :])

    predeep[0] = deep_taps(0, 1) + deep_taps(0, 2)
    predeep[1] = deep_taps(1, 0) + deep_taps(1, 1)

    def slopes(i, c):
        slope_mid[i] = 0.125 * act_slope(pre_mid[i])
        return c

    lax.fori_loop(0, 4, slopes, 0)

    loads[3].wait()

    grow = lax.broadcasted_iota(jnp.int32, (256, 256), 0) % 16

    def put_grad(i, value):
        pf[8:264, :] = value
        gcat[i, 16:272, 0:256] = jnp.where(grow == 15, 0.0, pf[9:265, :]).astype(BF)
        gcat[i, 16:272, 256:512] = value.astype(BF)
        gcat[i, 16:272, 512:768] = jnp.where(grow == 0, 0.0, pf[7:263, :]).astype(BF)

    def back_taps(plane, a):
        total = None
        for b in range(3):
            for c in range(3):
                rows = 16 * (2 - b)
                tap = (a * 3 + b) * 3 + c
                term = dot(
                    gcat[plane, rows : rows + 256, 256 * c : 256 * c + 256],
                    kd_ref[tap * 128 : (tap + 1) * 128, :],
                    ((1,), (1,)),
                )
                total = term if total is None else total + term
        return total

    b_copies = []
    for plane in (1, 0):
        p_copies[1 - plane].wait()
        if plane == 1:
            put_pooled(3, jnp.where(s == NS - 1, 0.0, phalo[1].astype(F32)))
        else:
            put_pooled(0, jnp.where(s == 0, 0.0, phalo[0].astype(F32)))
        pre = predeep[plane] + deep_taps(plane, 0 if plane == 0 else 2)
        predeep[plane] = pre
        value = (cot_ref[plane].astype(F32) * act_slope(pre)).astype(BF)
        grad[plane] = value
        put_grad(plane, value.astype(F32))
        bsend[plane] = back_taps(plane, 0 if plane == 0 else 2).astype(BF)
        b_copies.append(
            send(
                bsend.at[plane], bhalo.at[1 - plane], halo_send.at[4 + plane],
                halo_recv.at[4 + plane], {"space": down if plane == 0 else up},
            )
        )

    gown = grad[...].reshape(512, 256)
    for a in range(3):
        term = jnp.concatenate([
            dot(pcat[a, 16 * b : 16 * b + 256, :], gown[:256], ((0,), (0,))) + dot(pcat[a + 1, 16 * b : 16 * b + 256, :], gown[256:], ((0,), (0,)))
            for b in range(3)], axis=0).astype(BF).reshape(9, 128, 256)
        dbuf[0, 9 * a : 9 * a + 9] = term[:, :, :128]
        dbuf[1, 9 * a : 9 * a + 9] = term[:, :, 128:]
    d_pair = send(dbuf.at[1 - core], drecv1, pair_send.at[0], pair_recv.at[0], {"dp": other})

    back = [back_taps(0, 1) + back_taps(1, 0), back_taps(1, 1) + back_taps(0, 2)]

    d_pair.wait()
    dsum = (dbuf[core].astype(F32) + drecv1[...].astype(F32)).astype(BF)

    @pl.when(first_core)
    def _():
        for place in range(4):
            dsum1[place, 0:864, :] = dsum[:, 32 * place : 32 * place + 32, :].reshape(864, 128)
            dsum1[place, 864:896, :] = jnp.zeros((32, 128), BF)

    @pl.when(jnp.logical_not(first_core))
    def _():
        for place in range(4):
            taps = 7 if place < 3 else 6
            dsum1[place, 0 : taps * 128, :] = dsum[7 * place : 7 * place + taps].reshape(taps * 128, 128)
        dsum1[3, 768:896, :] = jnp.zeros((128, 128), BF)

    d_ring = []
    for k in range(1, 4):
        place, device = ring_peer(k)
        d_ring.append(send(dsum1.at[place], drecv2.at[k], ds_send.at[k], ds_recv.at[k], device))

    for plane in (1, 0):
        b_copies[plane].wait()
        edge = s == (0 if plane == 0 else NS - 1)
        total = back[plane] + jnp.where(edge, 0.0, bhalo[plane].astype(F32))
        total = total.astype(BF).astype(F32)
        wide = jnp.concatenate([total, total], axis=1).reshape(16, 1, 16, 256)
        for i in range(2):
            value = slope_mid[2 * plane + i].reshape(16, 2, 16, 256) * wide
            row = (2 * plane + i) * 512
            gmid[row : row + 512, :] = value.reshape(512, 256).astype(BF)

    def mid_grad(a):
        for b in range(3):
            cells = jnp.concatenate(
                [xpad[i + a, 16 * b : 16 * b + 512, :] for i in range(4)], axis=0
            )
            r = dot(cells, gmid[...], ((0,), (0,)))
            row = (a * 3 + b) * 192
            mbuf[row : row + 64, :] = (r[0:64, 128:] + r[192:256, :128]).astype(BF)
            mbuf[row + 64 : row + 128, :] = (r[0:64, :128] + r[64:128, 128:]).astype(BF)
            mbuf[row + 128 : row + 192, :] = (r[64:128, :128] + r[128:192, 128:]).astype(BF)

    def m_pair(p):
        base, rows = MPARTS[p]
        half = rows // 2
        theirs = pl.multiple_of(base + (1 - core) * half, 16)
        return send(
            mbuf.at[pl.ds(theirs, half), :], mrecv1.at[base // 2 : base // 2 + half, :],
            mp_send.at[p], mp_recv.at[p], {"dp": other},
        )

    def m_space(p, pair):
        base, rows = MPARTS[p]
        half, one = rows // 2, rows // 2 // NS
        lo = base // 2
        pair.wait()
        mine = pl.multiple_of(base + core * half, 16)
        msum1[lo : lo + half, :] = (
            mbuf[pl.ds(mine, half), :].astype(F32) + mrecv1[lo : lo + half, :].astype(F32)
        ).astype(BF)
        copies = []
        for k in range(1, NS):
            row = pl.multiple_of(lo + space_peer(k) * one, 16)
            copies.append(
                send(
                    msum1.at[pl.ds(row, one), :], mrecv2.at[k, lo // NS : lo // NS + one, :],
                    ms_send.at[p, k], ms_recv.at[p, k], {"space": space_peer(k)},
                )
            )
        return copies

    def m_dp(p, copies):
        base, rows = MPARTS[p]
        one = rows // 2 // NS
        lo = base // 2
        for copy in copies:
            copy.wait()
        row = pl.multiple_of(lo + s * one, 16)
        total = msum1[pl.ds(row, one), :].astype(F32)
        for k in range(1, NS):
            total = total + mrecv2[k, lo // NS : lo // NS + one, :].astype(F32)
        part = mrecv3.at[q, lo // NS : lo // NS + one, :]
        part[...] = total.astype(BF)
        return [
            send(part, part, mq_send.at[p, k], mq_recv.at[p, k], {"dp": dp_peer(k)})
            for k in range(1, NQ)
        ]

    def m_gather(p, copies):
        base, rows = MPARTS[p]
        one = rows // 2 // NS
        lo = base // 2
        for copy in copies:
            copy.wait()
        total = mrecv3[0, lo // NS : lo // NS + one, :].astype(F32)
        for k in range(1, NQ):
            total = total + mrecv3[k, lo // NS : lo // NS + one, :].astype(F32)
        row = pl.multiple_of(lo + s * one, 16)
        mfull[pl.ds(row, one), :] = total.astype(BF)
        part = mfull.at[pl.ds(row, one), :]
        return [
            send(part, part, mg_send.at[p, k], mg_recv.at[p, k], {"space": space_peer(k)})
            for k in range(1, NS)
        ]

    def m_last(p, copies):
        base, rows = MPARTS[p]
        half = rows // 2
        lo = base // 2
        for copy in copies:
            copy.wait()
        copy = send(
            mfull.at[lo : lo + half, :], mout.at[lo : lo + half, :], mo_send.at[p], mo_recv.at[p],
            {"dp": other},
        )
        mk_ref[pl.ds(pl.multiple_of(base + core * half, 16), half), :] = mfull[lo : lo + half, :]
        return copy

    def m_store(p, copy):
        base, rows = MPARTS[p]
        half = rows // 2
        lo = base // 2
        copy.wait()
        theirs = pl.multiple_of(base + (1 - core) * half, 16)
        mk_ref[pl.ds(theirs, half), :] = mout[lo : lo + half, :]

    mid_grad(0)
    m0 = m_pair(0)
    mid_grad(1)
    m1 = m_pair(1)
    m0 = m_space(0, m0)
    mid_grad(2)
    m2 = m_pair(2)
    m1 = m_space(1, m1)
    m2 = m_space(2, m2)

    out_ref[...] = act(predeep[...]).astype(BF)

    m0 = m_dp(0, m0)
    m1 = m_dp(1, m1)

    for copy in d_ring:
        copy.wait()
    total = dsum1[ring].astype(F32)
    for k in range(1, 4):
        total = total + drecv2[k].astype(F32)
    total = total.astype(BF)

    @pl.when(first_core)
    def _():
        rows = total.reshape(28, 2, 16, 128)
        for a in range(2):
            for b in range(7):
                dsum2[a * 8 + b] = rows[4 * b : 4 * b + 4, a].reshape(64, 128)
            dsum2[a * 8 + 7] = jnp.zeros((64, 128), BF)

    @pl.when(jnp.logical_not(first_core))
    def _():
        rows = total.reshape(7, 8, 16, 128)
        for a in range(8):
            dsum2[a * 2] = rows[0:4, a].reshape(64, 128)
            dsum2[a * 2 + 1, 0:48, :] = rows[4:7, a].reshape(48, 128)
            dsum2[a * 2 + 1, 48:64, :] = jnp.zeros((16, 128), BF)

    d_plane = []
    for k in range(1, 16):
        place, device = plane_peer(k)
        d_plane.append(send(dsum2.at[place], drecv3.at[k], dq_send.at[k], dq_recv.at[k], device))

    m2 = m_dp(2, m2)
    m0 = m_gather(0, m0)
    m1 = m_gather(1, m1)

    for copy in d_plane:
        copy.wait()
    total = dsum2[plane_peer(0)[0]].astype(F32)
    for k in range(1, 16):
        total = total + drecv3[k].astype(F32)
    dfull[q] = total.astype(BF)
    d_gather = [
        send(dfull.at[q], dfull.at[q], dg_send.at[k], dg_recv.at[k], {"dp": dp_peer(k)})
        for k in range(1, NQ)
    ]

    m2 = m_gather(2, m2)
    m0 = m_last(0, m0)
    m1 = m_last(1, m1)
    m_store(0, m0)
    m_store(1, m1)
    m2 = m_last(2, m2)
    for copy in d_gather:
        copy.wait()
    d_last = send(dfull, dother, pair_send.at[1], pair_recv.at[1], {"dp": other})
    m_store(2, m2)
    d_last.wait()
    left = jnp.where(first_core, dfull[...], dother[...]).reshape(NQ * DPIECE, 128)
    dk_ref[:, 0:128] = left[0:DROWS]
    right = jnp.where(first_core, dother[...], dfull[...])
    for place in range(4):
        row = 7 * 16 * place
        dk_ref[row : row + 64, 128:256] = right[place]
        rest = 48 if place < 3 else 32
        dk_ref[row + 64 : row + 64 + rest, 128:256] = right[4 + place, 0:rest]


def finish(deep_ref, dk_ref, mk_ref, out_ref, dg_ref, mg_ref):
    deep_scale = math.sqrt(NQ * 2 * NS * 2 * 256)
    mid_scale = math.sqrt(NQ * 2 * NS * 4 * 1024)
    out_ref[...] = deep_ref[...]
    dg_ref[...] = dk_ref[...].astype(F32) * (1.0 / deep_scale)
    mg_ref[...] = mk_ref[0 : 27 * 64, :].astype(F32) * (1.0 / mid_scale)


def on_device(volume, first_kernel, mid_kernel, deep_kernel, deep_cotangent):
    vm = pl.BlockSpec(memory_space=pltpu.VMEM)
    hbm = pl.BlockSpec(memory_space=pltpu.HBM)
    dma = pltpu.SemaphoreType.DMA
    deep_out, deep_grad, mid_grad = pl.pallas_call(
        kernel,
        out_shape=(
            jax.ShapeDtypeStruct((2, 256, 256), BF),
            jax.ShapeDtypeStruct((DROWS, 256), BF),
            jax.ShapeDtypeStruct((MROWS, 128), BF),
        ),
        in_specs=[vm] + [hbm] * 4,
        out_specs=(vm, vm, vm),
        scratch_shapes=[
            pltpu.VMEM((4, 32, 128), BF),
            pltpu.VMEM((27 * 64, 128), BF),
            pltpu.VMEM((27 * 128, 256), BF),
            pltpu.VMEM((2, 256, 256), BF),
            pltpu.VMEM((2, 2, 32, 128), BF),
            pltpu.VMEM((48, 128), F32),
            pltpu.VMEM((144, 128), F32),
            pltpu.VMEM((3, 256, 128), BF),
            pltpu.VMEM((1152, 2048), BF),
            pltpu.VMEM((192, 2048), F32),
            pltpu.VMEM((2, 512, 128), F32),
            pltpu.VMEM((2304, 256), BF),
            pltpu.VMEM((6, 544, 256), BF),
            pltpu.VMEM((4, 512, 256), F32),
            pltpu.VMEM((4, 512, 256), F32),
            pltpu.VMEM((2, 256, 128), BF),
            pltpu.VMEM((272, 256), F32),
            pltpu.VMEM((4, 288, 384), BF),
            pltpu.VMEM((2, 256, 128), BF),
            pltpu.VMEM((2, 256, 256), F32),
            pltpu.VMEM((2, 256, 256), BF),
            pltpu.VMEM((2, 256, 128), BF),
            pltpu.VMEM((2, 256, 128), BF),
            pltpu.VMEM((2, 288, 768), BF),
            pltpu.VMEM((2, 27, 128, 128), BF),
            pltpu.VMEM((27, 128, 128), BF),
            pltpu.VMEM((4, DQUARTER, 128), BF),
            pltpu.VMEM((4, DQUARTER, 128), BF),
            pltpu.VMEM((16, DPIECE, 128), BF),
            pltpu.VMEM((16, DPIECE, 128), BF),
            pltpu.VMEM((NQ, DPIECE, 128), BF),
            pltpu.VMEM((NQ, DPIECE, 128), BF),
            pltpu.VMEM((2048, 256), BF),
            pltpu.VMEM((MROWS, 128), BF),
            pltpu.VMEM((MHALF, 128), BF),
            pltpu.VMEM((MHALF, 128), BF),
            pltpu.VMEM((NS, MONE, 128), BF),
            pltpu.VMEM((NQ, MONE, 128), BF),
            pltpu.VMEM((MHALF, 128), BF),
            pltpu.VMEM((MHALF, 128), BF),
            dma((4,)), dma((6,)), dma((6,)), dma((2,)), dma((2,)),
            dma((4,)), dma((4,)), dma((16,)), dma((16,)), dma((8,)), dma((8,)),
            dma((3,)), dma((3,)),
            *[dma((3, 8)) for _ in range(6)],
            dma((3,)), dma((3,)),
        ],
        compiler_params=pltpu.CompilerParams(
            collective_id=0, has_side_effects=True, vmem_limit_bytes=44 * 1024 * 1024
        ),
    )(
        *[pltpu.with_memory_space_constraint(x, pltpu.HBM) for x in (first_kernel.reshape(27, 4, 64),
        volume[0],
        mid_kernel.reshape(27 * 64, 128),
        deep_kernel.reshape(27 * 128, 256),
        deep_cotangent.reshape(2, 256, 256))],
    )
    deep_out, deep_grad, mid_grad = pl.pallas_call(
        finish,
        out_shape=(
            jax.ShapeDtypeStruct((2, 256, 256), BF),
            jax.ShapeDtypeStruct((DROWS, 256), F32),
            jax.ShapeDtypeStruct((27 * 64, 128), F32),
        ),
        in_specs=[vm] * 3,
        out_specs=(vm, vm, vm),
        compiler_params=pltpu.CompilerParams(vmem_limit_bytes=8 * 1024 * 1024),
    )(deep_out, deep_grad, mid_grad)
    return (
        deep_out.reshape(1, 2, 16, 16, 256),
        deep_grad.reshape(3, 3, 3, CS, 256),
        mid_grad.reshape(3, 3, 3, 64, 128),
    )


def solution(mesh):
    in_specs = (P("dp", "space", None, None), P(), P(), P(), P("dp", "space", None, None, None))
    out_specs = (P("dp", "space", None, None, None), P(None, None, None, "space", None), P())
    return jax.shard_map(
        on_device, mesh=mesh, in_specs=in_specs, out_specs=out_specs, check_vma=False
    )
```

```python
import functools
import math

import jax
import jax.numpy as jnp
from jax import lax
from jax.experimental import pallas as pl
from jax.experimental.pallas import tpu as pltpu
from jax.sharding import PartitionSpec as P

SLOPE = 0.3
BF = jnp.bfloat16
F32 = jnp.float32
MESH = pl.DeviceIdType.MESH

NS = 8
NQ = 8
CS = 128 // NS
DROWS = 27 * CS
DPIECE = 64
DQUARTER = 28 * 32
MROWS = 28 * 64
MHALF = MROWS // 2
MPARTS = ((0, 512), (512, 512), (1024, 768))
MONE = MHALF // NS


def sigmoid(z):
    return 0.5 * jnp.tanh(0.5 * z) + 0.5


def act(z):
    return z * (SLOPE + (1.0 - SLOPE) * sigmoid(z))


def act_slope(z):
    s = sigmoid(z)
    return SLOPE + (1.0 - SLOPE) * (s + z * s * (1.0 - s))


def dot(a, b, dims=((1,), (0,))):
    return lax.dot_general(a, b, (dims, ((), ())), preferred_element_type=F32)


def kernel(
    fk_ref, vol_hbm, km_hbm, kd_hbm, cot_hbm,
    out_ref, dk_ref, mk_ref,
    vol_ref, km_ref, kd_ref, cot_ref,
    vhalo, ef, vf, volb, tmat, ybuf, yst, wmid, xpad, pre_mid, slope_mid,
    phalo, pf, pcat, pooled_send, predeep, grad, bsend, bhalo, gcat, dbuf, drecv1, dsum1,
    drecv2, dsum2, drecv3, dfull, dother, gmid, mbuf, mrecv1, msum1, mrecv2,
    mrecv3, mfull, mout,
    known, load_sem, halo_send, halo_recv, pair_send, pair_recv, ds_send, ds_recv, dq_send, dq_recv,
    dg_send, dg_recv, mp_send, mp_recv, ms_send, ms_recv, mq_send, mq_recv, mg_send, mg_recv,
    mo_send, mo_recv,
):
    s = lax.axis_index("space")
    d = lax.axis_index("dp")
    q = d // 2
    core = d % 2
    other = d + 1 - 2 * core

    def space_peer(k):
        return lax.rem(s + k, NS)

    def dp_peer(k):
        return lax.rem(q + k, NQ) * 2 + core

    first_core = core == 0
    y_low = s % 2
    z_chip = s // 2
    x_chip = q % 4
    y_high = q // 4
    ring = jnp.where(first_core, z_chip, x_chip)

    def ring_peer(k):
        place = lax.rem(ring + k, 4)
        return place, {
            "dp": jnp.where(first_core, d, (y_high * 4 + place) * 2 + core),
            "space": jnp.where(first_core, place * 2 + y_low, s),
        }

    def plane_peer(k):
        a = jnp.where(first_core, lax.rem(y_low + k // 8, 2), lax.rem(s + k // 2, 8))
        b = jnp.where(first_core, lax.rem(q + k % 8, 8), lax.rem(y_high + k % 2, 2))
        return jnp.where(first_core, a * 8 + b, a * 2 + b), {
            "dp": jnp.where(first_core, b, b * 4 + x_chip) * 2 + core,
            "space": jnp.where(first_core, z_chip * 2 + a, a),
        }

    up = space_peer(1)
    down = space_peer(NS - 1)

    barrier = pltpu.get_barrier_semaphore()
    near = [{"space": up}, {"space": down}]
    near += [{"space": lax.rem(s + k, NS)} for k in (2, NS - 2)]
    near += [{"dp": (y_high * 4 + lax.rem(x_chip + k, 4)) * 2 + core} for k in (1, 3)]
    near += [{"dp": lax.rem(q + 4, NQ) * 2 + core}, {"dp": other}]

    def tell(sem):
        for device in near:
            pl.semaphore_signal(sem, inc=1, device_id=device, device_id_type=MESH)

    tell(barrier)

    loads = []
    for i, (src, dst) in enumerate(
        ((vol_hbm, vol_ref), (km_hbm, km_ref), (kd_hbm, kd_ref), (cot_hbm, cot_ref))
    ):
        loads.append(pltpu.make_async_copy(src, dst, load_sem.at[i]))
        loads[-1].start()

    def send(src, dst, ssem, rsem, device):
        copy = pltpu.make_async_remote_copy(
            src_ref=src, dst_ref=dst, send_sem=ssem, recv_sem=rsem,
            device_id=device, device_id_type=MESH,
        )
        copy.start()
        return copy

    def zero_t(i, c):
        tmat[pl.ds(i * 16, 16), :] = jnp.zeros((16, 2048), BF)
        return c

    lax.fori_loop(0, 72, zero_t, 0)
    ef[...] = jnp.zeros((48, 128), F32)
    for ab in range(9):
        base = ab * 128
        for c in range(3):
            tap = fk_ref[ab * 3 + c].astype(F32)
            ef[16 + 4 * c : 20 + 4 * c, 0:64] = tap
            ef[20 + 4 * c : 24 + 4 * c, 64:128] = tap
        tiles = [ef[o : o + 16, :].astype(BF) for o in (4, 20, 12, 28)]
        for m in range(8):
            lo = slice(2 * m * 128, 2 * m * 128 + 128)
            hi = slice(2 * m * 128 + 128, 2 * m * 128 + 256)
            if m > 0:
                tmat[base + 16 * (m - 1) : base + 16 * m, lo] = tiles[0]
            tmat[base + 16 * m : base + 16 * m + 16, lo] = tiles[1]
            tmat[base + 16 * m : base + 16 * m + 16, hi] = tiles[2]
            if m < 7:
                tmat[base + 16 * (m + 1) : base + 16 * (m + 2), hi] = tiles[3]

    loads[0].wait()
    pl.semaphore_wait(barrier, len(near))

    v_down = send(vol_ref.at[0:2], vhalo.at[1], halo_send.at[0], halo_recv.at[0], {"space": down})
    v_up = send(vol_ref.at[2:4], vhalo.at[0], halo_send.at[1], halo_recv.at[1], {"space": up})

    tell(known.at[0])

    loads[1].wait()
    for ab in range(9):
        k0 = km_ref[(ab * 3) * 64 : (ab * 3 + 1) * 64, :]
        k1 = km_ref[(ab * 3 + 1) * 64 : (ab * 3 + 2) * 64, :]
        k2 = km_ref[(ab * 3 + 2) * 64 : (ab * 3 + 3) * 64, :]
        z = jnp.zeros((64, 128), BF)
        base = ab * 256
        wmid[base : base + 64, 0:128] = k1
        wmid[base : base + 64, 128:256] = k0
        wmid[base + 64 : base + 128, 0:128] = k2
        wmid[base + 64 : base + 128, 128:256] = k1
        wmid[base + 128 : base + 192, 0:128] = z
        wmid[base + 128 : base + 192, 128:256] = k2
        wmid[base + 192 : base + 256, 0:128] = k0
        wmid[base + 192 : base + 256, 128:256] = z
    for i in range(6):
        xpad[i, 0:16, :] = jnp.zeros((16, 256), BF)
        xpad[i, 528:544, :] = jnp.zeros((16, 256), BF)
    for i in range(4):
        pcat[i, 0:16, :] = jnp.zeros((16, 384), BF)
        pcat[i, 272:288, :] = jnp.zeros((16, 384), BF)
    for i in range(2):
        gcat[i, 0:16, :] = jnp.zeros((16, 768), BF)
        gcat[i, 272:288, :] = jnp.zeros((16, 768), BF)
    mbuf[27 * 64 : 28 * 64, :] = jnp.zeros((64, 128), BF)

    def put_volume(row, value):
        rows = value.shape[0]
        edge = lax.broadcasted_iota(jnp.int32, (rows, 128), 0) % 32
        vf[8 : 8 + rows, :] = value
        volb[0, row : row + rows, :] = jnp.where(edge == 0, 0.0, vf[7 : 7 + rows, :]).astype(BF)
        volb[1, row : row + rows, :] = value.astype(BF)
        volb[2, row : row + rows, :] = jnp.where(edge == 31, 0.0, vf[9 : 9 + rows, :]).astype(BF)

    vf[0:8, :] = jnp.zeros((8, 128), F32)
    vf[136:144, :] = jnp.zeros((8, 128), F32)
    put_volume(64, vol_ref[...].astype(F32).reshape(128, 128))

    def first(plane):
        def step(m, c):
            lhs = jnp.concatenate(
                [
                    volb[b, 32 * (plane + a) : 32 * (plane + a) + 64, :]
                    for a in range(3)
                    for b in range(3)
                ],
                axis=1,
            )
            col = pl.multiple_of(m * 256, 256)
            ybuf[32 * plane : 32 * plane + 64, pl.ds(col, 256)] = act(
                dot(lhs, tmat[:, pl.ds(col, 256)])
            )
            return c

        lax.fori_loop(0, 8, step, 0)

    lane = lax.broadcasted_iota(jnp.int32, (32, 128), 1)
    zero = jnp.zeros((32, 128), F32)

    def put_hidden(i):
        ys = [ybuf[32 * i : 32 * i + 32, 128 * j : 128 * j + 128] for j in range(16)]
        for j in range(16):
            after = ys[j + 1] if j < 15 else zero
            before = ys[j - 1] if j > 0 else zero
            yst[0, pl.ds(j, 32, stride=16), :] = ys[j]
            yst[1, pl.ds(j, 32, stride=16), :] = jnp.where(lane < 64, after, before)
        xpad[i, 16:528, 0:128] = yst[0].astype(BF)
        xpad[i, 16:528, 128:256] = yst[1].astype(BF)

    first(2)
    put_hidden(2)
    put_hidden(3)

    pl.semaphore_wait(known.at[0], len(near))
    tell(known.at[1])
    v_up.wait()
    put_volume(0, jnp.where(s == 0, 0.0, vhalo[0].astype(F32)).reshape(64, 128))
    first(0)
    ybuf[0:32, :] = jnp.where(s == 0, 0.0, ybuf[0:32, :])
    put_hidden(0)
    put_hidden(1)

    prow = lax.broadcasted_iota(jnp.int32, (256, 128), 0) % 16
    pf[0:8, :] = jnp.zeros((8, 256), F32)
    pf[264:272, :] = jnp.zeros((8, 256), F32)

    def put_pooled(i, value):
        pf[8:264, 0:128] = value
        pcat[i, 16:272, 0:128] = jnp.where(prow == 0, 0.0, pf[7:263, 0:128]).astype(BF)
        pcat[i, 16:272, 128:256] = value.astype(BF)
        pcat[i, 16:272, 256:384] = jnp.where(prow == 15, 0.0, pf[9:265, 0:128]).astype(BF)

    def mid_plane(i):
        lhs = jnp.concatenate(
            [xpad[i + a, 16 * b : 16 * b + 512, :] for a in range(3) for b in range(3)], axis=1
        )
        pre = dot(lhs, wmid[...])
        pre_mid[i] = pre
        value = act(pre).reshape(16, 2, 16, 256)
        value = value[:, 0] + value[:, 1]
        return (value[:, :, :128] + value[:, :, 128:]).reshape(256, 128)

    p_copies = []

    def pool(plane):
        pooled = ((mid_plane(2 * plane) + mid_plane(2 * plane + 1)) * 0.125).astype(BF)
        pooled_send[plane] = pooled
        p_copies.append(
            send(
                pooled_send.at[plane], phalo.at[1 - plane], halo_send.at[2 + plane],
                halo_recv.at[2 + plane], {"space": down if plane == 0 else up},
            )
        )
        put_pooled(plane + 1, pooled.astype(F32))

    pool(0)

    v_down.wait()
    put_volume(192, jnp.where(s == NS - 1, 0.0, vhalo[1].astype(F32)).reshape(64, 128))
    first(4)
    ybuf[160:192, :] = jnp.where(s == NS - 1, 0.0, ybuf[160:192, :])
    put_hidden(4)
    put_hidden(5)
    pool(1)

    pl.semaphore_wait(known.at[1], len(near))
    tell(known.at[2])
    loads[2].wait()

    def deep_taps(plane, a):
        lhs = jnp.concatenate(
            [pcat[plane + a, 16 * b : 16 * b + 256, :] for b in range(3)], axis=1
        )
        return dot(lhs, kd_ref[a * 1152 : (a + 1) * 1152, :])

    predeep[0] = deep_taps(0, 1) + deep_taps(0, 2)
    predeep[1] = deep_taps(1, 0) + deep_taps(1, 1)

    def slopes(i, c):
        slope_mid[i] = 0.125 * act_slope(pre_mid[i])
        return c

    lax.fori_loop(0, 4, slopes, 0)

    loads[3].wait()

    grow = lax.broadcasted_iota(jnp.int32, (256, 256), 0) % 16

    def put_grad(i, value):
        pf[8:264, :] = value
        gcat[i, 16:272, 0:256] = jnp.where(grow == 15, 0.0, pf[9:265, :]).astype(BF)
        gcat[i, 16:272, 256:512] = value.astype(BF)
        gcat[i, 16:272, 512:768] = jnp.where(grow == 0, 0.0, pf[7:263, :]).astype(BF)

    def back_taps(plane, a):
        total = None
        for b in range(3):
            for c in range(3):
                rows = 16 * (2 - b)
                tap = (a * 3 + b) * 3 + c
                term = dot(
                    gcat[plane, rows : rows + 256, 256 * c : 256 * c + 256],
                    kd_ref[tap * 128 : (tap + 1) * 128, :],
                    ((1,), (1,)),
                )
                total = term if total is None else total + term
        return total

    b_copies = []
    for plane in (1, 0):
        p_copies[1 - plane].wait()
        if plane == 1:
            put_pooled(3, jnp.where(s == NS - 1, 0.0, phalo[1].astype(F32)))
        else:
            put_pooled(0, jnp.where(s == 0, 0.0, phalo[0].astype(F32)))
        pre = predeep[plane] + deep_taps(plane, 0 if plane == 0 else 2)
        predeep[plane] = pre
        value = (cot_ref[plane].astype(F32) * act_slope(pre)).astype(BF)
        grad[plane] = value
        put_grad(plane, value.astype(F32))
        bsend[plane] = back_taps(plane, 0 if plane == 0 else 2).astype(BF)
        b_copies.append(
            send(
                bsend.at[plane], bhalo.at[1 - plane], halo_send.at[4 + plane],
                halo_recv.at[4 + plane], {"space": down if plane == 0 else up},
            )
        )

    gown = grad[...].reshape(512, 256)
    for a in range(3):
        term = jnp.concatenate([
            dot(pcat[a, 16 * b : 16 * b + 256, :], gown[:256], ((0,), (0,))) + dot(pcat[a + 1, 16 * b : 16 * b + 256, :], gown[256:], ((0,), (0,)))
            for b in range(3)], axis=0).astype(BF).reshape(9, 128, 256)
        dbuf[0, 9 * a : 9 * a + 9] = term[:, :, :128]
        dbuf[1, 9 * a : 9 * a + 9] = term[:, :, 128:]
    pl.semaphore_wait(known.at[2], len(near))
    d_pair = send(dbuf.at[1 - core], drecv1, pair_send.at[0], pair_recv.at[0], {"dp": other})

    back = [back_taps(0, 1) + back_taps(1, 0), back_taps(1, 1) + back_taps(0, 2)]

    d_pair.wait()
    dsum = (dbuf[core].astype(F32) + drecv1[...].astype(F32)).astype(BF)

    @pl.when(first_core)
    def _():
        for place in range(4):
            dsum1[place, 0:864, :] = dsum[:, 32 * place : 32 * place + 32, :].reshape(864, 128)
            dsum1[place, 864:896, :] = jnp.zeros((32, 128), BF)

    @pl.when(jnp.logical_not(first_core))
    def _():
        for place in range(4):
            taps = 7 if place < 3 else 6
            dsum1[place, 0 : taps * 128, :] = dsum[7 * place : 7 * place + taps].reshape(taps * 128, 128)
        dsum1[3, 768:896, :] = jnp.zeros((128, 128), BF)

    d_ring = []
    for k in range(1, 4):
        place, device = ring_peer(k)
        d_ring.append(send(dsum1.at[place], drecv2.at[k], ds_send.at[k], ds_recv.at[k], device))

    for plane in (1, 0):
        b_copies[plane].wait()
        edge = s == (0 if plane == 0 else NS - 1)
        total = back[plane] + jnp.where(edge, 0.0, bhalo[plane].astype(F32))
        total = total.astype(BF).astype(F32)
        wide = jnp.concatenate([total, total], axis=1).reshape(16, 1, 16, 256)
        for i in range(2):
            value = slope_mid[2 * plane + i].reshape(16, 2, 16, 256) * wide
            row = (2 * plane + i) * 512
            gmid[row : row + 512, :] = value.reshape(512, 256).astype(BF)

    def mid_grad(a):
        for b in range(3):
            cells = jnp.concatenate(
                [xpad[i + a, 16 * b : 16 * b + 512, :] for i in range(4)], axis=0
            )
            r = dot(cells, gmid[...], ((0,), (0,)))
            row = (a * 3 + b) * 192
            mbuf[row : row + 64, :] = (r[0:64, 128:] + r[192:256, :128]).astype(BF)
            mbuf[row + 64 : row + 128, :] = (r[0:64, :128] + r[64:128, 128:]).astype(BF)
            mbuf[row + 128 : row + 192, :] = (r[64:128, :128] + r[128:192, 128:]).astype(BF)

    def m_pair(p):
        base, rows = MPARTS[p]
        half = rows // 2
        theirs = pl.multiple_of(base + (1 - core) * half, 16)
        return send(
            mbuf.at[pl.ds(theirs, half), :], mrecv1.at[base // 2 : base // 2 + half, :],
            mp_send.at[p], mp_recv.at[p], {"dp": other},
        )

    def m_space(p, pair):
        base, rows = MPARTS[p]
        half, one = rows // 2, rows // 2 // NS
        lo = base // 2
        pair.wait()
        mine = pl.multiple_of(base + core * half, 16)
        msum1[lo : lo + half, :] = (
            mbuf[pl.ds(mine, half), :].astype(F32) + mrecv1[lo : lo + half, :].astype(F32)
        ).astype(BF)
        copies = []
        for k in range(1, NS):
            row = pl.multiple_of(lo + space_peer(k) * one, 16)
            copies.append(
                send(
                    msum1.at[pl.ds(row, one), :], mrecv2.at[k, lo // NS : lo // NS + one, :],
                    ms_send.at[p, k], ms_recv.at[p, k], {"space": space_peer(k)},
                )
            )
        return copies

    def m_dp(p, copies):
        base, rows = MPARTS[p]
        one = rows // 2 // NS
        lo = base // 2
        for copy in copies:
            copy.wait()
        row = pl.multiple_of(lo + s * one, 16)
        total = msum1[pl.ds(row, one), :].astype(F32)
        for k in range(1, NS):
            total = total + mrecv2[k, lo // NS : lo // NS + one, :].astype(F32)
        part = mrecv3.at[q, lo // NS : lo // NS + one, :]
        part[...] = total.astype(BF)
        return [
            send(part, part, mq_send.at[p, k], mq_recv.at[p, k], {"dp": dp_peer(k)})
            for k in range(1, NQ)
        ]

    def m_gather(p, copies):
        base, rows = MPARTS[p]
        one = rows // 2 // NS
        lo = base // 2
        for copy in copies:
            copy.wait()
        total = mrecv3[0, lo // NS : lo // NS + one, :].astype(F32)
        for k in range(1, NQ):
            total = total + mrecv3[k, lo // NS : lo // NS + one, :].astype(F32)
        row = pl.multiple_of(lo + s * one, 16)
        mfull[pl.ds(row, one), :] = total.astype(BF)
        part = mfull.at[pl.ds(row, one), :]
        return [
            send(part, part, mg_send.at[p, k], mg_recv.at[p, k], {"space": space_peer(k)})
            for k in range(1, NS)
        ]

    def m_last(p, copies):
        base, rows = MPARTS[p]
        half = rows // 2
        lo = base // 2
        for copy in copies:
            copy.wait()
        copy = send(
            mfull.at[lo : lo + half, :], mout.at[lo : lo + half, :], mo_send.at[p], mo_recv.at[p],
            {"dp": other},
        )
        mk_ref[pl.ds(pl.multiple_of(base + core * half, 16), half), :] = mfull[lo : lo + half, :]
        return copy

    def m_store(p, copy):
        base, rows = MPARTS[p]
        half = rows // 2
        lo = base // 2
        copy.wait()
        theirs = pl.multiple_of(base + (1 - core) * half, 16)
        mk_ref[pl.ds(theirs, half), :] = mout[lo : lo + half, :]

    mid_grad(0)
    m0 = m_pair(0)
    mid_grad(1)
    m1 = m_pair(1)
    m0 = m_space(0, m0)
    mid_grad(2)
    m2 = m_pair(2)
    m1 = m_space(1, m1)
    m2 = m_space(2, m2)

    out_ref[...] = act(predeep[...]).astype(BF)

    m0 = m_dp(0, m0)
    m1 = m_dp(1, m1)

    for copy in d_ring:
        copy.wait()
    total = dsum1[ring].astype(F32)
    for k in range(1, 4):
        total = total + drecv2[k].astype(F32)
    total = total.astype(BF)

    @pl.when(first_core)
    def _():
        rows = total.reshape(28, 2, 16, 128)
        for a in range(2):
            for b in range(7):
                dsum2[a * 8 + b] = rows[4 * b : 4 * b + 4, a].reshape(64, 128)
            dsum2[a * 8 + 7] = jnp.zeros((64, 128), BF)

    @pl.when(jnp.logical_not(first_core))
    def _():
        rows = total.reshape(7, 8, 16, 128)
        for a in range(8):
            dsum2[a * 2] = rows[0:4, a].reshape(64, 128)
            dsum2[a * 2 + 1, 0:48, :] = rows[4:7, a].reshape(48, 128)
            dsum2[a * 2 + 1, 48:64, :] = jnp.zeros((16, 128), BF)

    d_plane = []
    for k in range(1, 16):
        place, device = plane_peer(k)
        d_plane.append(send(dsum2.at[place], drecv3.at[k], dq_send.at[k], dq_recv.at[k], device))

    m2 = m_dp(2, m2)
    m0 = m_gather(0, m0)
    m1 = m_gather(1, m1)

    for copy in d_plane:
        copy.wait()
    total = dsum2[plane_peer(0)[0]].astype(F32)
    for k in range(1, 16):
        total = total + drecv3[k].astype(F32)
    dfull[q] = total.astype(BF)
    d_gather = [
        send(dfull.at[q], dfull.at[q], dg_send.at[k], dg_recv.at[k], {"dp": dp_peer(k)})
        for k in range(1, NQ)
    ]

    m2 = m_gather(2, m2)
    m0 = m_last(0, m0)
    m1 = m_last(1, m1)
    m_store(0, m0)
    m_store(1, m1)
    m2 = m_last(2, m2)
    for copy in d_gather:
        copy.wait()
    d_last = send(dfull, dother, pair_send.at[1], pair_recv.at[1], {"dp": other})
    m_store(2, m2)
    d_last.wait()
    left = jnp.where(first_core, dfull[...], dother[...]).reshape(NQ * DPIECE, 128)
    dk_ref[:, 0:128] = left[0:DROWS]
    right = jnp.where(first_core, dother[...], dfull[...])
    for place in range(4):
        row = 7 * 16 * place
        dk_ref[row : row + 64, 128:256] = right[place]
        rest = 48 if place < 3 else 32
        dk_ref[row + 64 : row + 64 + rest, 128:256] = right[4 + place, 0:rest]


def finish(deep_ref, dk_ref, mk_ref, out_ref, dg_ref, mg_ref):
    deep_scale = math.sqrt(NQ * 2 * NS * 2 * 256)
    mid_scale = math.sqrt(NQ * 2 * NS * 4 * 1024)
    out_ref[...] = deep_ref[...]
    dg_ref[...] = dk_ref[...].astype(F32) * (1.0 / deep_scale)
    mg_ref[...] = mk_ref[0 : 27 * 64, :].astype(F32) * (1.0 / mid_scale)


def on_device(volume, first_kernel, mid_kernel, deep_kernel, deep_cotangent):
    vm = pl.BlockSpec(memory_space=pltpu.VMEM)
    hbm = pl.BlockSpec(memory_space=pltpu.HBM)
    dma = pltpu.SemaphoreType.DMA
    deep_out, deep_grad, mid_grad = pl.pallas_call(
        kernel,
        out_shape=(
            jax.ShapeDtypeStruct((2, 256, 256), BF),
            jax.ShapeDtypeStruct((DROWS, 256), BF),
            jax.ShapeDtypeStruct((MROWS, 128), BF),
        ),
        in_specs=[vm] + [hbm] * 4,
        out_specs=(vm, vm, vm),
        scratch_shapes=[
            pltpu.VMEM((4, 32, 128), BF),
            pltpu.VMEM((27 * 64, 128), BF),
            pltpu.VMEM((27 * 128, 256), BF),
            pltpu.VMEM((2, 256, 256), BF),
            pltpu.VMEM((2, 2, 32, 128), BF),
            pltpu.VMEM((48, 128), F32),
            pltpu.VMEM((144, 128), F32),
            pltpu.VMEM((3, 256, 128), BF),
            pltpu.VMEM((1152, 2048), BF),
            pltpu.VMEM((192, 2048), F32),
            pltpu.VMEM((2, 512, 128), F32),
            pltpu.VMEM((2304, 256), BF),
            pltpu.VMEM((6, 544, 256), BF),
            pltpu.VMEM((4, 512, 256), F32),
            pltpu.VMEM((4, 512, 256), F32),
            pltpu.VMEM((2, 256, 128), BF),
            pltpu.VMEM((272, 256), F32),
            pltpu.VMEM((4, 288, 384), BF),
            pltpu.VMEM((2, 256, 128), BF),
            pltpu.VMEM((2, 256, 256), F32),
            pltpu.VMEM((2, 256, 256), BF),
            pltpu.VMEM((2, 256, 128), BF),
            pltpu.VMEM((2, 256, 128), BF),
            pltpu.VMEM((2, 288, 768), BF),
            pltpu.VMEM((2, 27, 128, 128), BF),
            pltpu.VMEM((27, 128, 128), BF),
            pltpu.VMEM((4, DQUARTER, 128), BF),
            pltpu.VMEM((4, DQUARTER, 128), BF),
            pltpu.VMEM((16, DPIECE, 128), BF),
            pltpu.VMEM((16, DPIECE, 128), BF),
            pltpu.VMEM((NQ, DPIECE, 128), BF),
            pltpu.VMEM((NQ, DPIECE, 128), BF),
            pltpu.VMEM((2048, 256), BF),
            pltpu.VMEM((MROWS, 128), BF),
            pltpu.VMEM((MHALF, 128), BF),
            pltpu.VMEM((MHALF, 128), BF),
            pltpu.VMEM((NS, MONE, 128), BF),
            pltpu.VMEM((NQ, MONE, 128), BF),
            pltpu.VMEM((MHALF, 128), BF),
            pltpu.VMEM((MHALF, 128), BF),
            pltpu.SemaphoreType.REGULAR((3,)),
            dma((4,)), dma((6,)), dma((6,)), dma((2,)), dma((2,)),
            dma((4,)), dma((4,)), dma((16,)), dma((16,)), dma((8,)), dma((8,)),
            dma((3,)), dma((3,)),
            *[dma((3, 8)) for _ in range(6)],
            dma((3,)), dma((3,)),
        ],
        compiler_params=pltpu.CompilerParams(
            collective_id=0, has_side_effects=True, vmem_limit_bytes=44 * 1024 * 1024
        ),
    )(
        *[pltpu.with_memory_space_constraint(x, pltpu.HBM) for x in (first_kernel.reshape(27, 4, 64),
        volume[0],
        mid_kernel.reshape(27 * 64, 128),
        deep_kernel.reshape(27 * 128, 256),
        deep_cotangent.reshape(2, 256, 256))],
    )
    deep_out, deep_grad, mid_grad = pl.pallas_call(
        finish,
        out_shape=(
            jax.ShapeDtypeStruct((2, 256, 256), BF),
            jax.ShapeDtypeStruct((DROWS, 256), F32),
            jax.ShapeDtypeStruct((27 * 64, 128), F32),
        ),
        in_specs=[vm] * 3,
        out_specs=(vm, vm, vm),
        compiler_params=pltpu.CompilerParams(vmem_limit_bytes=8 * 1024 * 1024),
    )(deep_out, deep_grad, mid_grad)
    return (
        deep_out.reshape(1, 2, 16, 16, 256),
        deep_grad.reshape(3, 3, 3, CS, 256),
        mid_grad.reshape(3, 3, 3, 64, 128),
    )


def solution(mesh):
    in_specs = (P("dp", "space", None, None), P(), P(), P(), P("dp", "space", None, None, None))
    out_specs = (P("dp", "space", None, None, None), P(None, None, None, "space", None), P())
    return jax.shard_map(
        on_device, mesh=mesh, in_specs=in_specs, out_specs=out_specs, check_vma=False
    )
```

```python
import functools
import math

import jax
import jax.numpy as jnp
from jax import lax
from jax.experimental import pallas as pl
from jax.experimental.pallas import tpu as pltpu
from jax.sharding import PartitionSpec as P

SLOPE = 0.3
BF = jnp.bfloat16
F32 = jnp.float32
MESH = pl.DeviceIdType.MESH

NS = 8
NQ = 8
CS = 128 // NS
DROWS = 27 * CS
DPIECE = 64
DQUARTER = 28 * 32
MROWS = 28 * 64
MHALF = MROWS // 2
MPARTS = ((0, 512), (512, 512), (1024, 768))
MONE = MHALF // NS


def sigmoid(z):
    return 0.5 * jnp.tanh(0.5 * z) + 0.5


def act(z):
    return z * (SLOPE + (1.0 - SLOPE) * sigmoid(z))


def act_slope(z):
    s = sigmoid(z)
    return SLOPE + (1.0 - SLOPE) * (s + z * s * (1.0 - s))


def dot(a, b, dims=((1,), (0,))):
    return lax.dot_general(a, b, (dims, ((), ())), preferred_element_type=F32)


def kernel(
    fk_ref, vol_hbm, km_hbm, kd_hbm, cot_hbm,
    out_ref, dk_ref, mk_ref,
    vol_ref, km_ref, kd_ref, cot_ref,
    vhalo, ef, vf, volb, tmat, ybuf, yst, wmid, xpad, pre_mid, slope_mid,
    phalo, pf, pcat, pooled_send, predeep, grad, bsend, bhalo, gcat, dbuf, drecv1, dsum1,
    drecv2, dsum2, drecv3, dfull, dother, gmid, mbuf, mrecv1, msum1, mrecv2,
    mrecv3, mfull, mout,
    known, load_sem, halo_send, halo_recv, pair_send, pair_recv, ds_send, ds_recv, dq_send, dq_recv,
    dg_send, dg_recv, mp_send, mp_recv, ms_send, ms_recv, mq_send, mq_recv, mg_send, mg_recv,
    mo_send, mo_recv,
):
    s = lax.axis_index("space")
    d = lax.axis_index("dp")
    q = d // 2
    core = d % 2
    other = d + 1 - 2 * core

    def space_peer(k):
        return lax.rem(s + k, NS)

    def dp_peer(k):
        return lax.rem(q + k, NQ) * 2 + core

    first_core = core == 0
    y_low = s % 2
    z_chip = s // 2
    x_chip = q % 4
    y_high = q // 4
    ring = jnp.where(first_core, z_chip, x_chip)

    def ring_peer(k):
        place = lax.rem(ring + k, 4)
        return place, {
            "dp": jnp.where(first_core, d, (y_high * 4 + place) * 2 + core),
            "space": jnp.where(first_core, place * 2 + y_low, s),
        }

    def plane_peer(k):
        a = jnp.where(first_core, lax.rem(y_low + k // 8, 2), lax.rem(s + k // 2, 8))
        b = jnp.where(first_core, lax.rem(q + k % 8, 8), lax.rem(y_high + k % 2, 2))
        return jnp.where(first_core, a * 8 + b, a * 2 + b), {
            "dp": jnp.where(first_core, b, b * 4 + x_chip) * 2 + core,
            "space": jnp.where(first_core, z_chip * 2 + a, a),
        }

    up = space_peer(1)
    down = space_peer(NS - 1)

    barrier = pltpu.get_barrier_semaphore()
    near = [{"space": up}, {"space": down}]
    near += [{"space": lax.rem(s + k, NS)} for k in (2, NS - 2)]
    near += [{"dp": (y_high * 4 + lax.rem(x_chip + k, 4)) * 2 + core} for k in (1, 3)]
    near += [{"dp": lax.rem(q + 4, NQ) * 2 + core}, {"dp": other}]

    def tell(sem):
        for device in near:
            pl.semaphore_signal(sem, inc=1, device_id=device, device_id_type=MESH)

    tell(barrier)

    loads = []
    for i, (src, dst) in enumerate(
        ((vol_hbm, vol_ref), (km_hbm, km_ref), (kd_hbm, kd_ref), (cot_hbm, cot_ref))
    ):
        loads.append(pltpu.make_async_copy(src, dst, load_sem.at[i]))
        loads[-1].start()

    def send(src, dst, ssem, rsem, device):
        copy = pltpu.make_async_remote_copy(
            src_ref=src, dst_ref=dst, send_sem=ssem, recv_sem=rsem,
            device_id=device, device_id_type=MESH,
        )
        copy.start()
        return copy

    def zero_t(i, c):
        tmat[pl.ds(i * 16, 16), :] = jnp.zeros((16, 2048), BF)
        return c

    lax.fori_loop(0, 72, zero_t, 0)
    ef[...] = jnp.zeros((48, 128), F32)
    for ab in range(9):
        base = ab * 128
        for c in range(3):
            tap = fk_ref[ab * 3 + c].astype(F32)
            ef[16 + 4 * c : 20 + 4 * c, 0:64] = tap
            ef[20 + 4 * c : 24 + 4 * c, 64:128] = tap
        tiles = [ef[o : o + 16, :].astype(BF) for o in (4, 20, 12, 28)]
        for m in range(8):
            lo = slice(2 * m * 128, 2 * m * 128 + 128)
            hi = slice(2 * m * 128 + 128, 2 * m * 128 + 256)
            if m > 0:
                tmat[base + 16 * (m - 1) : base + 16 * m, lo] = tiles[0]
            tmat[base + 16 * m : base + 16 * m + 16, lo] = tiles[1]
            tmat[base + 16 * m : base + 16 * m + 16, hi] = tiles[2]
            if m < 7:
                tmat[base + 16 * (m + 1) : base + 16 * (m + 2), hi] = tiles[3]

    loads[0].wait()
    pl.semaphore_wait(barrier, len(near))

    v_down = send(vol_ref.at[0:2], vhalo.at[1], halo_send.at[0], halo_recv.at[0], {"space": down})
    v_up = send(vol_ref.at[2:4], vhalo.at[0], halo_send.at[1], halo_recv.at[1], {"space": up})

    tell(known.at[0])

    loads[1].wait()
    for ab in range(9):
        k0 = km_ref[(ab * 3) * 64 : (ab * 3 + 1) * 64, :]
        k1 = km_ref[(ab * 3 + 1) * 64 : (ab * 3 + 2) * 64, :]
        k2 = km_ref[(ab * 3 + 2) * 64 : (ab * 3 + 3) * 64, :]
        z = jnp.zeros((64, 128), BF)
        base = ab * 256
        wmid[base : base + 64, 0:128] = k1
        wmid[base : base + 64, 128:256] = k0
        wmid[base + 64 : base + 128, 0:128] = k2
        wmid[base + 64 : base + 128, 128:256] = k1
        wmid[base + 128 : base + 192, 0:128] = z
        wmid[base + 128 : base + 192, 128:256] = k2
        wmid[base + 192 : base + 256, 0:128] = k0
        wmid[base + 192 : base + 256, 128:256] = z
    for i in range(6):
        xpad[i, 0:16, :] = jnp.zeros((16, 256), BF)
        xpad[i, 528:544, :] = jnp.zeros((16, 256), BF)
    for i in range(4):
        pcat[i, 0:16, :] = jnp.zeros((16, 384), BF)
        pcat[i, 272:288, :] = jnp.zeros((16, 384), BF)
    for i in range(2):
        gcat[i, 0:16, :] = jnp.zeros((16, 768), BF)
        gcat[i, 272:288, :] = jnp.zeros((16, 768), BF)
    mbuf[27 * 64 : 28 * 64, :] = jnp.zeros((64, 128), BF)

    def put_volume(row, value):
        rows = value.shape[0]
        edge = lax.broadcasted_iota(jnp.int32, (rows, 128), 0) % 32
        vf[8 : 8 + rows, :] = value
        volb[0, row : row + rows, :] = jnp.where(edge == 0, 0.0, vf[7 : 7 + rows, :]).astype(BF)
        volb[1, row : row + rows, :] = value.astype(BF)
        volb[2, row : row + rows, :] = jnp.where(edge == 31, 0.0, vf[9 : 9 + rows, :]).astype(BF)

    vf[0:8, :] = jnp.zeros((8, 128), F32)
    vf[136:144, :] = jnp.zeros((8, 128), F32)
    put_volume(64, vol_ref[...].astype(F32).reshape(128, 128))

    def first(plane):
        def step(m, c):
            lhs = jnp.concatenate(
                [
                    volb[b, 32 * (plane + a) : 32 * (plane + a) + 64, :]
                    for a in range(3)
                    for b in range(3)
                ],
                axis=1,
            )
            col = pl.multiple_of(m * 256, 256)
            ybuf[32 * plane : 32 * plane + 64, pl.ds(col, 256)] = act(
                dot(lhs, tmat[:, pl.ds(col, 256)])
            )
            return c

        lax.fori_loop(0, 8, step, 0)

    lane = lax.broadcasted_iota(jnp.int32, (32, 128), 1)
    zero = jnp.zeros((32, 128), F32)

    def put_hidden(i):
        ys = [ybuf[32 * i : 32 * i + 32, 128 * j : 128 * j + 128] for j in range(16)]
        for j in range(16):
            after = ys[j + 1] if j < 15 else zero
            before = ys[j - 1] if j > 0 else zero
            yst[0, pl.ds(j, 32, stride=16), :] = ys[j]
            yst[1, pl.ds(j, 32, stride=16), :] = jnp.where(lane < 64, after, before)
        xpad[i, 16:528, 0:128] = yst[0].astype(BF)
        xpad[i, 16:528, 128:256] = yst[1].astype(BF)

    first(2)
    put_hidden(2)
    put_hidden(3)

    pl.semaphore_wait(known.at[0], len(near))
    tell(known.at[1])
    v_up.wait()
    put_volume(0, jnp.where(s == 0, 0.0, vhalo[0].astype(F32)).reshape(64, 128))
    v_down.wait()
    put_volume(192, jnp.where(s == NS - 1, 0.0, vhalo[1].astype(F32)).reshape(64, 128))

    def outer(m, c):
        lhs = jnp.concatenate(
            [
                jnp.concatenate(
                    [volb[b, 32 * (p + a) : 32 * (p + a) + 64, :] for p in (0, 4)], axis=0
                )
                for a in range(3)
                for b in range(3)
            ],
            axis=1,
        )
        col = pl.multiple_of(m * 256, 256)
        value = act(dot(lhs, tmat[:, pl.ds(col, 256)]))
        ybuf[0:64, pl.ds(col, 256)] = value[0:64]
        ybuf[128:192, pl.ds(col, 256)] = value[64:128]
        return c

    lax.fori_loop(0, 8, outer, 0)
    ybuf[0:32, :] = jnp.where(s == 0, 0.0, ybuf[0:32, :])
    ybuf[160:192, :] = jnp.where(s == NS - 1, 0.0, ybuf[160:192, :])
    put_hidden(0)
    put_hidden(1)

    prow = lax.broadcasted_iota(jnp.int32, (256, 128), 0) % 16
    pf[0:8, :] = jnp.zeros((8, 256), F32)
    pf[264:272, :] = jnp.zeros((8, 256), F32)

    def put_pooled(i, value):
        pf[8:264, 0:128] = value
        pcat[i, 16:272, 0:128] = jnp.where(prow == 0, 0.0, pf[7:263, 0:128]).astype(BF)
        pcat[i, 16:272, 128:256] = value.astype(BF)
        pcat[i, 16:272, 256:384] = jnp.where(prow == 15, 0.0, pf[9:265, 0:128]).astype(BF)

    def mid_plane(i):
        lhs = jnp.concatenate(
            [xpad[i + a, 16 * b : 16 * b + 512, :] for a in range(3) for b in range(3)], axis=1
        )
        pre = dot(lhs, wmid[...])
        pre_mid[i] = pre
        value = act(pre).reshape(16, 2, 16, 256)
        value = value[:, 0] + value[:, 1]
        return (value[:, :, :128] + value[:, :, 128:]).reshape(256, 128)

    p_copies = []

    def pool(plane):
        pooled = ((mid_plane(2 * plane) + mid_plane(2 * plane + 1)) * 0.125).astype(BF)
        pooled_send[plane] = pooled
        p_copies.append(
            send(
                pooled_send.at[plane], phalo.at[1 - plane], halo_send.at[2 + plane],
                halo_recv.at[2 + plane], {"space": down if plane == 0 else up},
            )
        )
        put_pooled(plane + 1, pooled.astype(F32))

    pool(0)

    put_hidden(4)
    put_hidden(5)
    pool(1)

    pl.semaphore_wait(known.at[1], len(near))
    tell(known.at[2])
    loads[2].wait()

    def deep_taps(plane, a):
        lhs = jnp.concatenate(
            [pcat[plane + a, 16 * b : 16 * b + 256, :] for b in range(3)], axis=1
        )
        return dot(lhs, kd_ref[a * 1152 : (a + 1) * 1152, :])

    predeep[0] = deep_taps(0, 1) + deep_taps(0, 2)
    predeep[1] = deep_taps(1, 0) + deep_taps(1, 1)

    def slopes(i, c):
        slope_mid[i] = 0.125 * act_slope(pre_mid[i])
        return c

    lax.fori_loop(0, 4, slopes, 0)

    loads[3].wait()

    grow = lax.broadcasted_iota(jnp.int32, (256, 256), 0) % 16

    def put_grad(i, value):
        pf[8:264, :] = value
        gcat[i, 16:272, 0:256] = jnp.where(grow == 15, 0.0, pf[9:265, :]).astype(BF)
        gcat[i, 16:272, 256:512] = value.astype(BF)
        gcat[i, 16:272, 512:768] = jnp.where(grow == 0, 0.0, pf[7:263, :]).astype(BF)

    def back_taps(plane, a):
        total = None
        for b in range(3):
            for c in range(3):
                rows = 16 * (2 - b)
                tap = (a * 3 + b) * 3 + c
                term = dot(
                    gcat[plane, rows : rows + 256, 256 * c : 256 * c + 256],
                    kd_ref[tap * 128 : (tap + 1) * 128, :],
                    ((1,), (1,)),
                )
                total = term if total is None else total + term
        return total

    b_copies = []
    for plane in (1, 0):
        p_copies[1 - plane].wait()
        if plane == 1:
            put_pooled(3, jnp.where(s == NS - 1, 0.0, phalo[1].astype(F32)))
        else:
            put_pooled(0, jnp.where(s == 0, 0.0, phalo[0].astype(F32)))
        pre = predeep[plane] + deep_taps(plane, 0 if plane == 0 else 2)
        predeep[plane] = pre
        value = (cot_ref[plane].astype(F32) * act_slope(pre)).astype(BF)
        grad[plane] = value
        put_grad(plane, value.astype(F32))
        bsend[plane] = back_taps(plane, 0 if plane == 0 else 2).astype(BF)
        b_copies.append(
            send(
                bsend.at[plane], bhalo.at[1 - plane], halo_send.at[4 + plane],
                halo_recv.at[4 + plane], {"space": down if plane == 0 else up},
            )
        )

    gown = grad[...].reshape(512, 256)
    for a in range(3):
        term = jnp.concatenate([
            dot(pcat[a, 16 * b : 16 * b + 256, :], gown[:256], ((0,), (0,))) + dot(pcat[a + 1, 16 * b : 16 * b + 256, :], gown[256:], ((0,), (0,)))
            for b in range(3)], axis=0).astype(BF).reshape(9, 128, 256)
        dbuf[0, 9 * a : 9 * a + 9] = term[:, :, :128]
        dbuf[1, 9 * a : 9 * a + 9] = term[:, :, 128:]
    pl.semaphore_wait(known.at[2], len(near))
    d_pair = send(dbuf.at[1 - core], drecv1, pair_send.at[0], pair_recv.at[0], {"dp": other})

    back = [back_taps(0, 1) + back_taps(1, 0), back_taps(1, 1) + back_taps(0, 2)]

    d_pair.wait()
    dsum = (dbuf[core].astype(F32) + drecv1[...].astype(F32)).astype(BF)

    @pl.when(first_core)
    def _():
        for place in range(4):
            dsum1[place, 0:864, :] = dsum[:, 32 * place : 32 * place + 32, :].reshape(864, 128)
            dsum1[place, 864:896, :] = jnp.zeros((32, 128), BF)

    @pl.when(jnp.logical_not(first_core))
    def _():
        for place in range(4):
            taps = 7 if place < 3 else 6
            dsum1[place, 0 : taps * 128, :] = dsum[7 * place : 7 * place + taps].reshape(taps * 128, 128)
        dsum1[3, 768:896, :] = jnp.zeros((128, 128), BF)

    d_ring = []
    for k in range(1, 4):
        place, device = ring_peer(k)
        d_ring.append(send(dsum1.at[place], drecv2.at[k], ds_send.at[k], ds_recv.at[k], device))

    for plane in (1, 0):
        b_copies[plane].wait()
        edge = s == (0 if plane == 0 else NS - 1)
        total = back[plane] + jnp.where(edge, 0.0, bhalo[plane].astype(F32))
        total = total.astype(BF).astype(F32)
        wide = jnp.concatenate([total, total], axis=1).reshape(16, 1, 16, 256)
        for i in range(2):
            value = slope_mid[2 * plane + i].reshape(16, 2, 16, 256) * wide
            row = (2 * plane + i) * 512
            gmid[row : row + 512, :] = value.reshape(512, 256).astype(BF)

    def mid_grad(a):
        for b in range(3):
            cells = jnp.concatenate(
                [xpad[i + a, 16 * b : 16 * b + 512, :] for i in range(4)], axis=0
            )
            r = dot(cells, gmid[...], ((0,), (0,)))
            row = (a * 3 + b) * 192
            mbuf[row : row + 64, :] = (r[0:64, 128:] + r[192:256, :128]).astype(BF)
            mbuf[row + 64 : row + 128, :] = (r[0:64, :128] + r[64:128, 128:]).astype(BF)
            mbuf[row + 128 : row + 192, :] = (r[64:128, :128] + r[128:192, 128:]).astype(BF)

    def m_pair(p):
        base, rows = MPARTS[p]
        half = rows // 2
        theirs = pl.multiple_of(base + (1 - core) * half, 16)
        return send(
            mbuf.at[pl.ds(theirs, half), :], mrecv1.at[base // 2 : base // 2 + half, :],
            mp_send.at[p], mp_recv.at[p], {"dp": other},
        )

    def m_space(p, pair):
        base, rows = MPARTS[p]
        half, one = rows // 2, rows // 2 // NS
        lo = base // 2
        pair.wait()
        mine = pl.multiple_of(base + core * half, 16)
        msum1[lo : lo + half, :] = (
            mbuf[pl.ds(mine, half), :].astype(F32) + mrecv1[lo : lo + half, :].astype(F32)
        ).astype(BF)
        copies = []
        for k in range(1, NS):
            row = pl.multiple_of(lo + space_peer(k) * one, 16)
            copies.append(
                send(
                    msum1.at[pl.ds(row, one), :], mrecv2.at[k, lo // NS : lo // NS + one, :],
                    ms_send.at[p, k], ms_recv.at[p, k], {"space": space_peer(k)},
                )
            )
        return copies

    def m_dp(p, copies):
        base, rows = MPARTS[p]
        one = rows // 2 // NS
        lo = base // 2
        for copy in copies:
            copy.wait()
        row = pl.multiple_of(lo + s * one, 16)
        total = msum1[pl.ds(row, one), :].astype(F32)
        for k in range(1, NS):
            total = total + mrecv2[k, lo // NS : lo // NS + one, :].astype(F32)
        part = mrecv3.at[q, lo // NS : lo // NS + one, :]
        part[...] = total.astype(BF)
        return [
            send(part, part, mq_send.at[p, k], mq_recv.at[p, k], {"dp": dp_peer(k)})
            for k in range(1, NQ)
        ]

    def m_gather(p, copies):
        base, rows = MPARTS[p]
        one = rows // 2 // NS
        lo = base // 2
        for copy in copies:
            copy.wait()
        total = mrecv3[0, lo // NS : lo // NS + one, :].astype(F32)
        for k in range(1, NQ):
            total = total + mrecv3[k, lo // NS : lo // NS + one, :].astype(F32)
        row = pl.multiple_of(lo + s * one, 16)
        mfull[pl.ds(row, one), :] = total.astype(BF)
        part = mfull.at[pl.ds(row, one), :]
        return [
            send(part, part, mg_send.at[p, k], mg_recv.at[p, k], {"space": space_peer(k)})
            for k in range(1, NS)
        ]

    def m_last(p, copies):
        base, rows = MPARTS[p]
        half = rows // 2
        lo = base // 2
        for copy in copies:
            copy.wait()
        copy = send(
            mfull.at[lo : lo + half, :], mout.at[lo : lo + half, :], mo_send.at[p], mo_recv.at[p],
            {"dp": other},
        )
        mk_ref[pl.ds(pl.multiple_of(base + core * half, 16), half), :] = mfull[lo : lo + half, :]
        return copy

    def m_store(p, copy):
        base, rows = MPARTS[p]
        half = rows // 2
        lo = base // 2
        copy.wait()
        theirs = pl.multiple_of(base + (1 - core) * half, 16)
        mk_ref[pl.ds(theirs, half), :] = mout[lo : lo + half, :]

    mid_grad(0)
    m0 = m_pair(0)
    mid_grad(1)
    m1 = m_pair(1)
    m0 = m_space(0, m0)
    mid_grad(2)
    m2 = m_pair(2)
    m1 = m_space(1, m1)
    m2 = m_space(2, m2)

    out_ref[...] = act(predeep[...]).astype(BF)

    m0 = m_dp(0, m0)
    m1 = m_dp(1, m1)

    for copy in d_ring:
        copy.wait()
    total = dsum1[ring].astype(F32)
    for k in range(1, 4):
        total = total + drecv2[k].astype(F32)
    total = total.astype(BF)

    @pl.when(first_core)
    def _():
        rows = total.reshape(28, 2, 16, 128)
        for a in range(2):
            for b in range(7):
                dsum2[a * 8 + b] = rows[4 * b : 4 * b + 4, a].reshape(64, 128)
            dsum2[a * 8 + 7] = jnp.zeros((64, 128), BF)

    @pl.when(jnp.logical_not(first_core))
    def _():
        rows = total.reshape(7, 8, 16, 128)
        for a in range(8):
            dsum2[a * 2] = rows[0:4, a].reshape(64, 128)
            dsum2[a * 2 + 1, 0:48, :] = rows[4:7, a].reshape(48, 128)
            dsum2[a * 2 + 1, 48:64, :] = jnp.zeros((16, 128), BF)

    d_plane = []
    for k in range(1, 16):
        place, device = plane_peer(k)
        d_plane.append(send(dsum2.at[place], drecv3.at[k], dq_send.at[k], dq_recv.at[k], device))

    m2 = m_dp(2, m2)
    m0 = m_gather(0, m0)
    m1 = m_gather(1, m1)

    for copy in d_plane:
        copy.wait()
    total = dsum2[plane_peer(0)[0]].astype(F32)
    for k in range(1, 16):
        total = total + drecv3[k].astype(F32)
    dfull[q] = total.astype(BF)
    d_gather = [
        send(dfull.at[q], dfull.at[q], dg_send.at[k], dg_recv.at[k], {"dp": dp_peer(k)})
        for k in range(1, NQ)
    ]

    m2 = m_gather(2, m2)
    m0 = m_last(0, m0)
    m1 = m_last(1, m1)
    m_store(0, m0)
    m_store(1, m1)
    for copy in d_gather:
        copy.wait()
    d_last = send(dfull, dother, pair_send.at[1], pair_recv.at[1], {"dp": other})
    m2 = m_last(2, m2)
    d_last.wait()
    left = jnp.where(first_core, dfull[...], dother[...]).reshape(NQ * DPIECE, 128)
    dk_ref[:, 0:128] = left[0:DROWS]
    right = jnp.where(first_core, dother[...], dfull[...])
    for place in range(4):
        row = 7 * 16 * place
        dk_ref[row : row + 64, 128:256] = right[place]
        rest = 48 if place < 3 else 32
        dk_ref[row + 64 : row + 64 + rest, 128:256] = right[4 + place, 0:rest]
    m_store(2, m2)


def finish(deep_ref, dk_ref, mk_ref, out_ref, dg_ref, mg_ref):
    deep_scale = math.sqrt(NQ * 2 * NS * 2 * 256)
    mid_scale = math.sqrt(NQ * 2 * NS * 4 * 1024)
    out_ref[...] = deep_ref[...]
    dg_ref[...] = dk_ref[...].astype(F32) * (1.0 / deep_scale)
    mg_ref[...] = mk_ref[0 : 27 * 64, :].astype(F32) * (1.0 / mid_scale)


def on_device(volume, first_kernel, mid_kernel, deep_kernel, deep_cotangent):
    vm = pl.BlockSpec(memory_space=pltpu.VMEM)
    hbm = pl.BlockSpec(memory_space=pltpu.HBM)
    dma = pltpu.SemaphoreType.DMA
    deep_out, deep_grad, mid_grad = pl.pallas_call(
        kernel,
        out_shape=(
            jax.ShapeDtypeStruct((2, 256, 256), BF),
            jax.ShapeDtypeStruct((DROWS, 256), BF),
            jax.ShapeDtypeStruct((MROWS, 128), BF),
        ),
        in_specs=[vm] + [hbm] * 4,
        out_specs=(vm, vm, vm),
        scratch_shapes=[
            pltpu.VMEM((4, 32, 128), BF),
            pltpu.VMEM((27 * 64, 128), BF),
            pltpu.VMEM((27 * 128, 256), BF),
            pltpu.VMEM((2, 256, 256), BF),
            pltpu.VMEM((2, 2, 32, 128), BF),
            pltpu.VMEM((48, 128), F32),
            pltpu.VMEM((144, 128), F32),
            pltpu.VMEM((3, 256, 128), BF),
            pltpu.VMEM((1152, 2048), BF),
            pltpu.VMEM((192, 2048), F32),
            pltpu.VMEM((2, 512, 128), F32),
            pltpu.VMEM((2304, 256), BF),
            pltpu.VMEM((6, 544, 256), BF),
            pltpu.VMEM((4, 512, 256), F32),
            pltpu.VMEM((4, 512, 256), F32),
            pltpu.VMEM((2, 256, 128), BF),
            pltpu.VMEM((272, 256), F32),
            pltpu.VMEM((4, 288, 384), BF),
            pltpu.VMEM((2, 256, 128), BF),
            pltpu.VMEM((2, 256, 256), F32),
            pltpu.VMEM((2, 256, 256), BF),
            pltpu.VMEM((2, 256, 128), BF),
            pltpu.VMEM((2, 256, 128), BF),
            pltpu.VMEM((2, 288, 768), BF),
            pltpu.VMEM((2, 27, 128, 128), BF),
            pltpu.VMEM((27, 128, 128), BF),
            pltpu.VMEM((4, DQUARTER, 128), BF),
            pltpu.VMEM((4, DQUARTER, 128), BF),
            pltpu.VMEM((16, DPIECE, 128), BF),
            pltpu.VMEM((16, DPIECE, 128), BF),
            pltpu.VMEM((NQ, DPIECE, 128), BF),
            pltpu.VMEM((NQ, DPIECE, 128), BF),
            pltpu.VMEM((2048, 256), BF),
            pltpu.VMEM((MROWS, 128), BF),
            pltpu.VMEM((MHALF, 128), BF),
            pltpu.VMEM((MHALF, 128), BF),
            pltpu.VMEM((NS, MONE, 128), BF),
            pltpu.VMEM((NQ, MONE, 128), BF),
            pltpu.VMEM((MHALF, 128), BF),
            pltpu.VMEM((MHALF, 128), BF),
            pltpu.SemaphoreType.REGULAR((3,)),
            dma((4,)), dma((6,)), dma((6,)), dma((2,)), dma((2,)),
            dma((4,)), dma((4,)), dma((16,)), dma((16,)), dma((8,)), dma((8,)),
            dma((3,)), dma((3,)),
            *[dma((3, 8)) for _ in range(6)],
            dma((3,)), dma((3,)),
        ],
        compiler_params=pltpu.CompilerParams(
            collective_id=0, has_side_effects=True, vmem_limit_bytes=44 * 1024 * 1024
        ),
    )(
        *[pltpu.with_memory_space_constraint(x, pltpu.HBM) for x in (first_kernel.reshape(27, 4, 64),
        volume[0],
        mid_kernel.reshape(27 * 64, 128),
        deep_kernel.reshape(27 * 128, 256),
        deep_cotangent.reshape(2, 256, 256))],
    )
    deep_out, deep_grad, mid_grad = pl.pallas_call(
        finish,
        out_shape=(
            jax.ShapeDtypeStruct((2, 256, 256), BF),
            jax.ShapeDtypeStruct((DROWS, 256), F32),
            jax.ShapeDtypeStruct((27 * 64, 128), F32),
        ),
        in_specs=[vm] * 3,
        out_specs=(vm, vm, vm),
        compiler_params=pltpu.CompilerParams(vmem_limit_bytes=8 * 1024 * 1024),
    )(deep_out, deep_grad, mid_grad)
    return (
        deep_out.reshape(1, 2, 16, 16, 256),
        deep_grad.reshape(3, 3, 3, CS, 256),
        mid_grad.reshape(3, 3, 3, 64, 128),
    )


def solution(mesh):
    in_specs = (P("dp", "space", None, None), P(), P(), P(), P("dp", "space", None, None, None))
    out_specs = (P("dp", "space", None, None, None), P(None, None, None, "space", None), P())
    return jax.shard_map(
        on_device, mesh=mesh, in_specs=in_specs, out_specs=out_specs, check_vma=False
    )
```

```python
import functools
import math

import jax
import jax.numpy as jnp
from jax import lax
from jax.experimental import pallas as pl
from jax.experimental.pallas import tpu as pltpu
from jax.sharding import PartitionSpec as P

SLOPE = 0.3
BF = jnp.bfloat16
F32 = jnp.float32
MESH = pl.DeviceIdType.MESH

NS = 8
NQ = 8
CS = 128 // NS
DROWS = 27 * CS
DPIECE = 64
DQUARTER = 28 * 32
MROWS = 28 * 64
MHALF = MROWS // 2
MPARTS = ((0, 512), (512, 512), (1024, 768))
MONE = MHALF // NS


def sigmoid(z):
    return 0.5 * jnp.tanh(0.5 * z) + 0.5


def act(z):
    return z * (SLOPE + (1.0 - SLOPE) * sigmoid(z))


def act_slope(z):
    s = sigmoid(z)
    return SLOPE + (1.0 - SLOPE) * (s + z * s * (1.0 - s))


def dot(a, b, dims=((1,), (0,))):
    return lax.dot_general(a, b, (dims, ((), ())), preferred_element_type=F32)


def kernel(
    fk_ref, vol_hbm, km_hbm, kd_hbm, cot_hbm,
    out_ref, dk_ref, mk_ref,
    vol_ref, km_ref, kd_ref, cot_ref,
    vhalo, ef, vf, volb, tmat, ybuf, yst, wmid, xpad, pre_mid, slope_mid,
    phalo, pf, pcat, pooled_send, predeep, grad, bsend, bhalo, gcat, dbuf, drecv1, dsum1,
    drecv2, dsum2, drecv3, dfull, dother, gmid, mbuf, mrecv1, msum1, mrecv2,
    mrecv3, mfull, mout,
    known, load_sem, halo_send, halo_recv, pair_send, pair_recv, ds_send, ds_recv, dq_send, dq_recv,
    dg_send, dg_recv, mp_send, mp_recv, ms_send, ms_recv, mq_send, mq_recv, mg_send, mg_recv,
    mo_send, mo_recv,
):
    s = lax.axis_index("space")
    d = lax.axis_index("dp")
    q = d // 2
    core = d % 2
    other = d + 1 - 2 * core

    def space_peer(k):
        return lax.rem(s + k, NS)

    def dp_peer(k):
        return lax.rem(q + k, NQ) * 2 + core

    first_core = core == 0
    y_low = s % 2
    z_chip = s // 2
    x_chip = q % 4
    y_high = q // 4
    ring = jnp.where(first_core, z_chip, x_chip)

    def ring_peer(k):
        place = lax.rem(ring + k, 4)
        return place, {
            "dp": jnp.where(first_core, d, (y_high * 4 + place) * 2 + core),
            "space": jnp.where(first_core, place * 2 + y_low, s),
        }

    def plane_peer(k):
        a = jnp.where(first_core, lax.rem(y_low + k // 8, 2), lax.rem(s + k // 2, 8))
        b = jnp.where(first_core, lax.rem(q + k % 8, 8), lax.rem(y_high + k % 2, 2))
        return jnp.where(first_core, a * 8 + b, a * 2 + b), {
            "dp": jnp.where(first_core, b, b * 4 + x_chip) * 2 + core,
            "space": jnp.where(first_core, z_chip * 2 + a, a),
        }

    up = space_peer(1)
    down = space_peer(NS - 1)

    barrier = pltpu.get_barrier_semaphore()
    near = [{"space": up}, {"space": down}]
    near += [{"space": lax.rem(s + k, NS)} for k in (2, NS - 2)]
    near += [{"dp": (y_high * 4 + lax.rem(x_chip + k, 4)) * 2 + core} for k in (1, 3)]
    near += [{"dp": lax.rem(q + 4, NQ) * 2 + core}, {"dp": other}]

    def tell(sem):
        for device in near:
            pl.semaphore_signal(sem, inc=1, device_id=device, device_id_type=MESH)

    tell(barrier)

    loads = []
    for i, (src, dst) in enumerate(
        ((vol_hbm, vol_ref), (km_hbm, km_ref), (kd_hbm, kd_ref), (cot_hbm, cot_ref))
    ):
        loads.append(pltpu.make_async_copy(src, dst, load_sem.at[i]))
        loads[-1].start()

    def send(src, dst, ssem, rsem, device):
        copy = pltpu.make_async_remote_copy(
            src_ref=src, dst_ref=dst, send_sem=ssem, recv_sem=rsem,
            device_id=device, device_id_type=MESH,
        )
        copy.start()
        return copy

    def zero_t(i, c):
        tmat[pl.ds(i * 16, 16), :] = jnp.zeros((16, 2048), BF)
        return c

    lax.fori_loop(0, 72, zero_t, 0)
    ef[...] = jnp.zeros((48, 128), F32)
    for ab in range(9):
        base = ab * 128
        for c in range(3):
            tap = fk_ref[ab * 3 + c].astype(F32)
            ef[16 + 4 * c : 20 + 4 * c, 0:64] = tap
            ef[20 + 4 * c : 24 + 4 * c, 64:128] = tap
        tiles = [ef[o : o + 16, :].astype(BF) for o in (4, 20, 12, 28)]
        for m in range(8):
            lo = slice(2 * m * 128, 2 * m * 128 + 128)
            hi = slice(2 * m * 128 + 128, 2 * m * 128 + 256)
            if m > 0:
                tmat[base + 16 * (m - 1) : base + 16 * m, lo] = tiles[0]
            tmat[base + 16 * m : base + 16 * m + 16, lo] = tiles[1]
            tmat[base + 16 * m : base + 16 * m + 16, hi] = tiles[2]
            if m < 7:
                tmat[base + 16 * (m + 1) : base + 16 * (m + 2), hi] = tiles[3]

    loads[0].wait()
    pl.semaphore_wait(barrier, len(near))

    v_down = send(vol_ref.at[0:2], vhalo.at[1], halo_send.at[0], halo_recv.at[0], {"space": down})
    v_up = send(vol_ref.at[2:4], vhalo.at[0], halo_send.at[1], halo_recv.at[1], {"space": up})

    tell(known.at[0])

    loads[1].wait()
    for ab in range(9):
        k0 = km_ref[(ab * 3) * 64 : (ab * 3 + 1) * 64, :]
        k1 = km_ref[(ab * 3 + 1) * 64 : (ab * 3 + 2) * 64, :]
        k2 = km_ref[(ab * 3 + 2) * 64 : (ab * 3 + 3) * 64, :]
        z = jnp.zeros((64, 128), BF)
        base = ab * 256
        wmid[base : base + 64, 0:128] = k1
        wmid[base : base + 64, 128:256] = k0
        wmid[base + 64 : base + 128, 0:128] = k2
        wmid[base + 64 : base + 128, 128:256] = k1
        wmid[base + 128 : base + 192, 0:128] = z
        wmid[base + 128 : base + 192, 128:256] = k2
        wmid[base + 192 : base + 256, 0:128] = k0
        wmid[base + 192 : base + 256, 128:256] = z
    for i in range(6):
        xpad[i, 0:16, :] = jnp.zeros((16, 256), BF)
        xpad[i, 528:544, :] = jnp.zeros((16, 256), BF)
    for i in range(4):
        pcat[i, 0:16, :] = jnp.zeros((16, 384), BF)
        pcat[i, 272:288, :] = jnp.zeros((16, 384), BF)
    for i in range(2):
        gcat[i, 0:16, :] = jnp.zeros((16, 768), BF)
        gcat[i, 272:288, :] = jnp.zeros((16, 768), BF)
    mbuf[27 * 64 : 28 * 64, :] = jnp.zeros((64, 128), BF)

    def put_volume(row, value):
        rows = value.shape[0]
        edge = lax.broadcasted_iota(jnp.int32, (rows, 128), 0) % 32
        vf[8 : 8 + rows, :] = value
        volb[0, row : row + rows, :] = jnp.where(edge == 0, 0.0, vf[7 : 7 + rows, :]).astype(BF)
        volb[1, row : row + rows, :] = value.astype(BF)
        volb[2, row : row + rows, :] = jnp.where(edge == 31, 0.0, vf[9 : 9 + rows, :]).astype(BF)

    vf[0:8, :] = jnp.zeros((8, 128), F32)
    vf[136:144, :] = jnp.zeros((8, 128), F32)
    put_volume(64, vol_ref[...].astype(F32).reshape(128, 128))

    def first(plane):
        def step(m, c):
            lhs = jnp.concatenate(
                [
                    volb[b, 32 * (plane + a) : 32 * (plane + a) + 64, :]
                    for a in range(3)
                    for b in range(3)
                ],
                axis=1,
            )
            col = pl.multiple_of(m * 256, 256)
            ybuf[32 * plane : 32 * plane + 64, pl.ds(col, 256)] = act(
                dot(lhs, tmat[:, pl.ds(col, 256)])
            )
            return c

        lax.fori_loop(0, 8, step, 0)

    lane = lax.broadcasted_iota(jnp.int32, (32, 128), 1)
    zero = jnp.zeros((32, 128), F32)

    def put_hidden(i):
        ys = [ybuf[32 * i : 32 * i + 32, 128 * j : 128 * j + 128] for j in range(16)]
        for j in range(16):
            after = ys[j + 1] if j < 15 else zero
            before = ys[j - 1] if j > 0 else zero
            yst[0, pl.ds(j, 32, stride=16), :] = ys[j]
            yst[1, pl.ds(j, 32, stride=16), :] = jnp.where(lane < 64, after, before)
        xpad[i, 16:528, 0:128] = yst[0].astype(BF)
        xpad[i, 16:528, 128:256] = yst[1].astype(BF)

    first(2)
    put_hidden(2)
    put_hidden(3)

    pl.semaphore_wait(known.at[0], len(near))
    tell(known.at[1])
    v_up.wait()
    put_volume(0, jnp.where(s == 0, 0.0, vhalo[0].astype(F32)).reshape(64, 128))
    v_down.wait()
    put_volume(192, jnp.where(s == NS - 1, 0.0, vhalo[1].astype(F32)).reshape(64, 128))

    def outer(m, c):
        lhs = jnp.concatenate(
            [
                jnp.concatenate(
                    [volb[b, 32 * (p + a) : 32 * (p + a) + 64, :] for p in (0, 4)], axis=0
                )
                for a in range(3)
                for b in range(3)
            ],
            axis=1,
        )
        col = pl.multiple_of(m * 256, 256)
        value = act(dot(lhs, tmat[:, pl.ds(col, 256)]))
        ybuf[0:64, pl.ds(col, 256)] = value[0:64]
        ybuf[128:192, pl.ds(col, 256)] = value[64:128]
        return c

    lax.fori_loop(0, 8, outer, 0)
    ybuf[0:32, :] = jnp.where(s == 0, 0.0, ybuf[0:32, :])
    ybuf[160:192, :] = jnp.where(s == NS - 1, 0.0, ybuf[160:192, :])
    put_hidden(0)
    put_hidden(1)

    prow = lax.broadcasted_iota(jnp.int32, (256, 128), 0) % 16
    pf[0:8, :] = jnp.zeros((8, 256), F32)
    pf[264:272, :] = jnp.zeros((8, 256), F32)

    def put_pooled(i, value):
        pf[8:264, 0:128] = value
        pcat[i, 16:272, 0:128] = jnp.where(prow == 0, 0.0, pf[7:263, 0:128]).astype(BF)
        pcat[i, 16:272, 128:256] = value.astype(BF)
        pcat[i, 16:272, 256:384] = jnp.where(prow == 15, 0.0, pf[9:265, 0:128]).astype(BF)

    def mid_plane(i):
        lhs = jnp.concatenate(
            [xpad[i + a, 16 * b : 16 * b + 512, :] for a in range(3) for b in range(3)], axis=1
        )
        pre = dot(lhs, wmid[...])
        pre_mid[i] = pre
        value = act(pre).reshape(16, 2, 16, 256)
        value = value[:, 0] + value[:, 1]
        return (value[:, :, :128] + value[:, :, 128:]).reshape(256, 128)

    p_copies = []

    def pool(plane):
        pooled = ((mid_plane(2 * plane) + mid_plane(2 * plane + 1)) * 0.125).astype(BF)
        pooled_send[plane] = pooled
        p_copies.append(
            send(
                pooled_send.at[plane], phalo.at[1 - plane], halo_send.at[2 + plane],
                halo_recv.at[2 + plane], {"space": down if plane == 0 else up},
            )
        )
        put_pooled(plane + 1, pooled.astype(F32))

    pool(0)

    put_hidden(4)
    put_hidden(5)
    pool(1)

    pl.semaphore_wait(known.at[1], len(near))
    tell(known.at[2])
    loads[2].wait()

    def deep_taps(plane, a):
        lhs = jnp.concatenate(
            [pcat[plane + a, 16 * b : 16 * b + 256, :] for b in range(3)], axis=1
        )
        return dot(lhs, kd_ref[a * 1152 : (a + 1) * 1152, :])

    predeep[0] = deep_taps(0, 1) + deep_taps(0, 2)
    predeep[1] = deep_taps(1, 0) + deep_taps(1, 1)

    def slopes(i, c):
        slope_mid[i] = 0.125 * act_slope(pre_mid[i])
        return c

    lax.fori_loop(0, 4, slopes, 0)

    loads[3].wait()

    grow = lax.broadcasted_iota(jnp.int32, (256, 256), 0) % 16

    def put_grad(i, value):
        pf[8:264, :] = value
        gcat[i, 16:272, 0:256] = jnp.where(grow == 15, 0.0, pf[9:265, :]).astype(BF)
        gcat[i, 16:272, 256:512] = value.astype(BF)
        gcat[i, 16:272, 512:768] = jnp.where(grow == 0, 0.0, pf[7:263, :]).astype(BF)

    def back_taps(plane, a):
        total = None
        for b in range(3):
            for c in range(3):
                rows = 16 * (2 - b)
                tap = (a * 3 + b) * 3 + c
                term = dot(
                    gcat[plane, rows : rows + 256, 256 * c : 256 * c + 256],
                    kd_ref[tap * 128 : (tap + 1) * 128, :],
                    ((1,), (1,)),
                )
                total = term if total is None else total + term
        return total

    b_copies = []
    for plane in (1, 0):
        p_copies[1 - plane].wait()
        if plane == 1:
            put_pooled(3, jnp.where(s == NS - 1, 0.0, phalo[1].astype(F32)))
        else:
            put_pooled(0, jnp.where(s == 0, 0.0, phalo[0].astype(F32)))
        pre = predeep[plane] + deep_taps(plane, 0 if plane == 0 else 2)
        predeep[plane] = pre
        value = (cot_ref[plane].astype(F32) * act_slope(pre)).astype(BF)
        grad[plane] = value
        put_grad(plane, value.astype(F32))
        bsend[plane] = back_taps(plane, 0 if plane == 0 else 2).astype(BF)
        b_copies.append(
            send(
                bsend.at[plane], bhalo.at[1 - plane], halo_send.at[4 + plane],
                halo_recv.at[4 + plane], {"space": down if plane == 0 else up},
            )
        )

    pl.semaphore_wait(known.at[2], len(near))
    gown = grad[...].reshape(512, 256)
    d_pair = []
    for a in range(3):
        term = jnp.concatenate([
            dot(pcat[a, 16 * b : 16 * b + 256, :], gown[:256], ((0,), (0,))) + dot(pcat[a + 1, 16 * b : 16 * b + 256, :], gown[256:], ((0,), (0,)))
            for b in range(3)], axis=0).astype(BF).reshape(9, 128, 256)
        dbuf[0, 9 * a : 9 * a + 9] = term[:, :, :128]
        dbuf[1, 9 * a : 9 * a + 9] = term[:, :, 128:]
        d_pair.append(
            send(
                dbuf.at[1 - core, 9 * a : 9 * a + 9], drecv1.at[9 * a : 9 * a + 9],
                pair_send.at[2 + a], pair_recv.at[2 + a], {"dp": other},
            )
        )

    for copy in d_pair:
        copy.wait()
    dsum = (dbuf[core].astype(F32) + drecv1[...].astype(F32)).astype(BF)

    @pl.when(first_core)
    def _():
        for place in range(4):
            dsum1[place, 0:864, :] = dsum[:, 32 * place : 32 * place + 32, :].reshape(864, 128)
            dsum1[place, 864:896, :] = jnp.zeros((32, 128), BF)

    @pl.when(jnp.logical_not(first_core))
    def _():
        for place in range(4):
            taps = 7 if place < 3 else 6
            dsum1[place, 0 : taps * 128, :] = dsum[7 * place : 7 * place + taps].reshape(taps * 128, 128)
        dsum1[3, 768:896, :] = jnp.zeros((128, 128), BF)

    d_ring = []
    for k in range(1, 4):
        place, device = ring_peer(k)
        d_ring.append(send(dsum1.at[place], drecv2.at[k], ds_send.at[k], ds_recv.at[k], device))

    back = [back_taps(0, 1) + back_taps(1, 0), back_taps(1, 1) + back_taps(0, 2)]

    for plane in (1, 0):
        b_copies[plane].wait()
        edge = s == (0 if plane == 0 else NS - 1)
        total = back[plane] + jnp.where(edge, 0.0, bhalo[plane].astype(F32))
        total = total.astype(BF).astype(F32)
        wide = jnp.concatenate([total, total], axis=1).reshape(16, 1, 16, 256)
        for i in range(2):
            value = slope_mid[2 * plane + i].reshape(16, 2, 16, 256) * wide
            row = (2 * plane + i) * 512
            gmid[row : row + 512, :] = value.reshape(512, 256).astype(BF)

    def mid_grad(a):
        for b in range(3):
            cells = jnp.concatenate(
                [xpad[i + a, 16 * b : 16 * b + 512, :] for i in range(4)], axis=0
            )
            r = dot(cells, gmid[...], ((0,), (0,)))
            row = (a * 3 + b) * 192
            mbuf[row : row + 64, :] = (r[0:64, 128:] + r[192:256, :128]).astype(BF)
            mbuf[row + 64 : row + 128, :] = (r[0:64, :128] + r[64:128, 128:]).astype(BF)
            mbuf[row + 128 : row + 192, :] = (r[64:128, :128] + r[128:192, 128:]).astype(BF)

    def m_pair(p):
        base, rows = MPARTS[p]
        half = rows // 2
        theirs = pl.multiple_of(base + (1 - core) * half, 16)
        return send(
            mbuf.at[pl.ds(theirs, half), :], mrecv1.at[base // 2 : base // 2 + half, :],
            mp_send.at[p], mp_recv.at[p], {"dp": other},
        )

    def m_space(p, pair):
        base, rows = MPARTS[p]
        half, one = rows // 2, rows // 2 // NS
        lo = base // 2
        pair.wait()
        mine = pl.multiple_of(base + core * half, 16)
        msum1[lo : lo + half, :] = (
            mbuf[pl.ds(mine, half), :].astype(F32) + mrecv1[lo : lo + half, :].astype(F32)
        ).astype(BF)
        copies = []
        for k in range(1, NS):
            row = pl.multiple_of(lo + space_peer(k) * one, 16)
            copies.append(
                send(
                    msum1.at[pl.ds(row, one), :], mrecv2.at[k, lo // NS : lo // NS + one, :],
                    ms_send.at[p, k], ms_recv.at[p, k], {"space": space_peer(k)},
                )
            )
        return copies

    def m_dp(p, copies):
        base, rows = MPARTS[p]
        one = rows // 2 // NS
        lo = base // 2
        for copy in copies:
            copy.wait()
        row = pl.multiple_of(lo + s * one, 16)
        total = msum1[pl.ds(row, one), :].astype(F32)
        for k in range(1, NS):
            total = total + mrecv2[k, lo // NS : lo // NS + one, :].astype(F32)
        part = mrecv3.at[q, lo // NS : lo // NS + one, :]
        part[...] = total.astype(BF)
        return [
            send(part, part, mq_send.at[p, k], mq_recv.at[p, k], {"dp": dp_peer(k)})
            for k in range(1, NQ)
        ]

    def m_gather(p, copies):
        base, rows = MPARTS[p]
        one = rows // 2 // NS
        lo = base // 2
        for copy in copies:
            copy.wait()
        total = mrecv3[0, lo // NS : lo // NS + one, :].astype(F32)
        for k in range(1, NQ):
            total = total + mrecv3[k, lo // NS : lo // NS + one, :].astype(F32)
        row = pl.multiple_of(lo + s * one, 16)
        mfull[pl.ds(row, one), :] = total.astype(BF)
        part = mfull.at[pl.ds(row, one), :]
        return [
            send(part, part, mg_send.at[p, k], mg_recv.at[p, k], {"space": space_peer(k)})
            for k in range(1, NS)
        ]

    def m_last(p, copies):
        base, rows = MPARTS[p]
        half = rows // 2
        lo = base // 2
        for copy in copies:
            copy.wait()
        copy = send(
            mfull.at[lo : lo + half, :], mout.at[lo : lo + half, :], mo_send.at[p], mo_recv.at[p],
            {"dp": other},
        )
        mk_ref[pl.ds(pl.multiple_of(base + core * half, 16), half), :] = mfull[lo : lo + half, :]
        return copy

    def m_store(p, copy):
        base, rows = MPARTS[p]
        half = rows // 2
        lo = base // 2
        copy.wait()
        theirs = pl.multiple_of(base + (1 - core) * half, 16)
        mk_ref[pl.ds(theirs, half), :] = mout[lo : lo + half, :]

    mid_grad(0)
    m0 = m_pair(0)
    mid_grad(1)
    m1 = m_pair(1)
    m0 = m_space(0, m0)
    mid_grad(2)
    m2 = m_pair(2)
    m1 = m_space(1, m1)
    m2 = m_space(2, m2)

    out_ref[...] = act(predeep[...]).astype(BF)

    m0 = m_dp(0, m0)
    m1 = m_dp(1, m1)

    for copy in d_ring:
        copy.wait()
    total = dsum1[ring].astype(F32)
    for k in range(1, 4):
        total = total + drecv2[k].astype(F32)
    total = total.astype(BF)

    @pl.when(first_core)
    def _():
        rows = total.reshape(28, 2, 16, 128)
        for a in range(2):
            for b in range(7):
                dsum2[a * 8 + b] = rows[4 * b : 4 * b + 4, a].reshape(64, 128)
            dsum2[a * 8 + 7] = jnp.zeros((64, 128), BF)

    @pl.when(jnp.logical_not(first_core))
    def _():
        rows = total.reshape(7, 8, 16, 128)
        for a in range(8):
            dsum2[a * 2] = rows[0:4, a].reshape(64, 128)
            dsum2[a * 2 + 1, 0:48, :] = rows[4:7, a].reshape(48, 128)
            dsum2[a * 2 + 1, 48:64, :] = jnp.zeros((16, 128), BF)

    d_plane = []
    for k in range(1, 16):
        place, device = plane_peer(k)
        d_plane.append(send(dsum2.at[place], drecv3.at[k], dq_send.at[k], dq_recv.at[k], device))

    m2 = m_dp(2, m2)
    m0 = m_gather(0, m0)
    m1 = m_gather(1, m1)

    for copy in d_plane:
        copy.wait()
    total = dsum2[plane_peer(0)[0]].astype(F32)
    for k in range(1, 16):
        total = total + drecv3[k].astype(F32)
    dfull[q] = total.astype(BF)
    d_gather = [
        send(dfull.at[q], dfull.at[q], dg_send.at[k], dg_recv.at[k], {"dp": dp_peer(k)})
        for k in range(1, NQ)
    ]

    m2 = m_gather(2, m2)
    m0 = m_last(0, m0)
    m1 = m_last(1, m1)
    m_store(0, m0)
    m_store(1, m1)
    for copy in d_gather:
        copy.wait()
    d_last = send(dfull, dother, pair_send.at[1], pair_recv.at[1], {"dp": other})
    m2 = m_last(2, m2)
    d_last.wait()
    left = jnp.where(first_core, dfull[...], dother[...]).reshape(NQ * DPIECE, 128)
    dk_ref[:, 0:128] = left[0:DROWS]
    right = jnp.where(first_core, dother[...], dfull[...])
    for place in range(4):
        row = 7 * 16 * place
        dk_ref[row : row + 64, 128:256] = right[place]
        rest = 48 if place < 3 else 32
        dk_ref[row + 64 : row + 64 + rest, 128:256] = right[4 + place, 0:rest]
    m_store(2, m2)


def finish(deep_ref, dk_ref, mk_ref, out_ref, dg_ref, mg_ref):
    deep_scale = math.sqrt(NQ * 2 * NS * 2 * 256)
    mid_scale = math.sqrt(NQ * 2 * NS * 4 * 1024)
    out_ref[...] = deep_ref[...]
    dg_ref[...] = dk_ref[...].astype(F32) * (1.0 / deep_scale)
    mg_ref[...] = mk_ref[0 : 27 * 64, :].astype(F32) * (1.0 / mid_scale)


def on_device(volume, first_kernel, mid_kernel, deep_kernel, deep_cotangent):
    vm = pl.BlockSpec(memory_space=pltpu.VMEM)
    hbm = pl.BlockSpec(memory_space=pltpu.HBM)
    dma = pltpu.SemaphoreType.DMA
    deep_out, deep_grad, mid_grad = pl.pallas_call(
        kernel,
        out_shape=(
            jax.ShapeDtypeStruct((2, 256, 256), BF),
            jax.ShapeDtypeStruct((DROWS, 256), BF),
            jax.ShapeDtypeStruct((MROWS, 128), BF),
        ),
        in_specs=[vm] + [hbm] * 4,
        out_specs=(vm, vm, vm),
        scratch_shapes=[
            pltpu.VMEM((4, 32, 128), BF),
            pltpu.VMEM((27 * 64, 128), BF),
            pltpu.VMEM((27 * 128, 256), BF),
            pltpu.VMEM((2, 256, 256), BF),
            pltpu.VMEM((2, 2, 32, 128), BF),
            pltpu.VMEM((48, 128), F32),
            pltpu.VMEM((144, 128), F32),
            pltpu.VMEM((3, 256, 128), BF),
            pltpu.VMEM((1152, 2048), BF),
            pltpu.VMEM((192, 2048), F32),
            pltpu.VMEM((2, 512, 128), F32),
            pltpu.VMEM((2304, 256), BF),
            pltpu.VMEM((6, 544, 256), BF),
            pltpu.VMEM((4, 512, 256), F32),
            pltpu.VMEM((4, 512, 256), F32),
            pltpu.VMEM((2, 256, 128), BF),
            pltpu.VMEM((272, 256), F32),
            pltpu.VMEM((4, 288, 384), BF),
            pltpu.VMEM((2, 256, 128), BF),
            pltpu.VMEM((2, 256, 256), F32),
            pltpu.VMEM((2, 256, 256), BF),
            pltpu.VMEM((2, 256, 128), BF),
            pltpu.VMEM((2, 256, 128), BF),
            pltpu.VMEM((2, 288, 768), BF),
            pltpu.VMEM((2, 27, 128, 128), BF),
            pltpu.VMEM((27, 128, 128), BF),
            pltpu.VMEM((4, DQUARTER, 128), BF),
            pltpu.VMEM((4, DQUARTER, 128), BF),
            pltpu.VMEM((16, DPIECE, 128), BF),
            pltpu.VMEM((16, DPIECE, 128), BF),
            pltpu.VMEM((NQ, DPIECE, 128), BF),
            pltpu.VMEM((NQ, DPIECE, 128), BF),
            pltpu.VMEM((2048, 256), BF),
            pltpu.VMEM((MROWS, 128), BF),
            pltpu.VMEM((MHALF, 128), BF),
            pltpu.VMEM((MHALF, 128), BF),
            pltpu.VMEM((NS, MONE, 128), BF),
            pltpu.VMEM((NQ, MONE, 128), BF),
            pltpu.VMEM((MHALF, 128), BF),
            pltpu.VMEM((MHALF, 128), BF),
            pltpu.SemaphoreType.REGULAR((3,)),
            dma((4,)), dma((6,)), dma((6,)), dma((5,)), dma((5,)),
            dma((4,)), dma((4,)), dma((16,)), dma((16,)), dma((8,)), dma((8,)),
            dma((3,)), dma((3,)),
            *[dma((3, 8)) for _ in range(6)],
            dma((3,)), dma((3,)),
        ],
        compiler_params=pltpu.CompilerParams(
            collective_id=0, has_side_effects=True, vmem_limit_bytes=44 * 1024 * 1024
        ),
    )(
        *[pltpu.with_memory_space_constraint(x, pltpu.HBM) for x in (first_kernel.reshape(27, 4, 64),
        volume[0],
        mid_kernel.reshape(27 * 64, 128),
        deep_kernel.reshape(27 * 128, 256),
        deep_cotangent.reshape(2, 256, 256))],
    )
    deep_out, deep_grad, mid_grad = pl.pallas_call(
        finish,
        out_shape=(
            jax.ShapeDtypeStruct((2, 256, 256), BF),
            jax.ShapeDtypeStruct((DROWS, 256), F32),
            jax.ShapeDtypeStruct((27 * 64, 128), F32),
        ),
        in_specs=[vm] * 3,
        out_specs=(vm, vm, vm),
        compiler_params=pltpu.CompilerParams(vmem_limit_bytes=8 * 1024 * 1024),
    )(deep_out, deep_grad, mid_grad)
    return (
        deep_out.reshape(1, 2, 16, 16, 256),
        deep_grad.reshape(3, 3, 3, CS, 256),
        mid_grad.reshape(3, 3, 3, 64, 128),
    )


def solution(mesh):
    in_specs = (P("dp", "space", None, None), P(), P(), P(), P("dp", "space", None, None, None))
    out_specs = (P("dp", "space", None, None, None), P(None, None, None, "space", None), P())
    return jax.shard_map(
        on_device, mesh=mesh, in_specs=in_specs, out_specs=out_specs, check_vma=False
    )
```
